32 devices in a mesh: span: 8 (over z, x), mix: 4 (over y, core).
Axes of the slice: x: 2, y: 2, z: 4, core: 2. Of those that a mesh axis runs over, the one named last changes fastest.
Arguments:
- audio: float32 [131072], P(('mix', 'span')), parts along dimension 0, may hold values from -6 to 6
- w_enc: float32 [16, 256], replicated, may hold values from -1.5 to 1.5
- intra_query: bfloat16 [256, 256], replicated, may hold values from -8 to 8, as said below
- intra_kv: bfloat16 [256, 512], replicated, may hold values from -8 to 8, as said below
- intra_out: bfloat16 [256, 256], replicated, may hold values from -0.375 to 0.375
- intra_up: bfloat16 [256, 1024], replicated, may hold values from -0.375 to 0.375
- intra_down: bfloat16 [1024, 256], replicated, may hold values from -0.1875 to 0.1875
- inter_query: bfloat16 [256, 256], replicated, may hold values from -8 to 8, as said below
- inter_kv: bfloat16 [256, 512], replicated, may hold values from -8 to 8, as said below
- inter_out: bfloat16 [256, 256], replicated, may hold values from -0.375 to 0.375
- inter_up: bfloat16 [256, 1024], replicated, may hold values from -0.375 to 0.375
- inter_down: bfloat16 [1024, 256], replicated, may hold values from -0.1875 to 0.1875
- w_mask: bfloat16 [256, 512], replicated, may hold values from -0.375 to 0.375
Outputs:
- separated: bfloat16 [16384, 512], P(('mix', 'span')), parts along dimension 0
The draws below stay inside these ranges and needn't reach their ends.
There are 4 independent parts, one for each index of `mix`. The reference program is written for one: setup_inputs(seed, part) draws one part's arguments, and reference() takes and returns one part's arrays. A program takes and returns all parts, laid end to end along the dimension named above; an argument that names none is the same for every part. Nothing has to cross between parts.
Inputs may be any that keep to these rules, and one draw needn't show every extreme that they name: `intra_query`: projection weights of the query. `intra_kv`: projection weights of keys and values. `inter_query`: projection weights of the query. `inter_kv`: projection weights of keys and values.
All inputs are finite; a program needn't handle non-finite values.
Results may differ from the reference program's by a relative error of at most 0.025.
Values may be sent and summed in bfloat16 or wider, within the bound.
A program may use at most 64 MiB of HBM per device.

```python
import math
import jax
import jax.numpy as jnp
from jax import lax

N = 256
FF = 1024
HEADS = 8
K = 256
HOP = 128
KERNEL = 16
STRIDE = 8
SPK = 2
SPANS = 32
FRAMES = 4096
SAMPLES = 32768


def pair_weights(key, salt):
    inner = jax.random.fold_in(key, salt)
    first_key, second_key = jax.random.split(inner, 2)
    score_scale = N ** (-0.5)
    kv_part = jax.random.normal(first_key, (N, 2 * N), jnp.float32) * score_scale
    noise = jax.random.normal(second_key, (N, N), jnp.float32) * score_scale
    query_part = noise
    return (jnp.clip(query_part, -8.0, 8.0), jnp.clip(kv_part, -8.0, 8.0))


def draw_intra_query(key, part):
    return pair_weights(key, 11)[0].astype(jnp.bfloat16)


def draw_intra_kv(key, part):
    return pair_weights(key, 11)[1].astype(jnp.bfloat16)


def draw_inter_query(key, part):
    return pair_weights(key, 23)[0].astype(jnp.bfloat16)


def draw_inter_kv(key, part):
    return pair_weights(key, 23)[1].astype(jnp.bfloat16)


def block_scale(key, shape, cuts, least, largest):
    gain = 1.0
    for position, blocks in cuts:
        heights = jax.random.uniform(jax.random.fold_in(jax.random.fold_in(key, 6), position), (blocks,), jnp.float32, least / len(cuts), largest / len(cuts))
        gain = gain * jnp.repeat(jnp.exp(heights), shape[position] // blocks).reshape((-1,) + (1,) * (len(shape) - 1 - position))
    return gain


def gaussian(stream_key, dims, scale, reach, cuts=(), kind=jnp.bfloat16):
    gain = block_scale(stream_key, dims, cuts, -0.22, 0.18) if cuts else 1.0
    drawn = jax.random.normal(stream_key, dims, jnp.float32) * scale * gain
    return jnp.minimum(jnp.maximum(drawn, -reach), reach).astype(kind)


def setup_inputs(seed: int = 0, part: int = 0) -> dict:
    key_of = jax.random.split(jax.random.key(seed), 14)
    own_keys = jax.random.split(jax.random.fold_in(key_of[13], part), 14)
    audio = gaussian(own_keys[0], (SAMPLES,), 1.0, 6.0, ((0, 8),), jnp.float32)
    w_enc = gaussian(key_of[1], (KERNEL, N), KERNEL ** -0.5, 1.5, (), jnp.float32)
    intra_query = draw_intra_query(jax.random.fold_in(key_of[13], 71), part)
    intra_kv = draw_intra_kv(jax.random.fold_in(key_of[13], 71), part)
    intra_out = gaussian(key_of[4], (N, N), N ** -0.5, 0.375)
    intra_up = gaussian(key_of[5], (N, FF), N ** -0.5, 0.375)
    intra_down = gaussian(key_of[6], (FF, N), FF ** -0.5, 0.1875)
    inter_query = draw_inter_query(jax.random.fold_in(key_of[13], 71), part)
    inter_kv = draw_inter_kv(jax.random.fold_in(key_of[13], 71), part)
    inter_out = gaussian(key_of[9], (N, N), N ** -0.5, 0.375)
    inter_up = gaussian(key_of[10], (N, FF), N ** -0.5, 0.375)
    inter_down = gaussian(key_of[11], (FF, N), FF ** -0.5, 0.1875)
    w_mask = gaussian(key_of[12], (N, SPK * N), N ** -0.5, 0.375)
    return {"audio": audio, "w_enc": w_enc, "intra_query": intra_query, "intra_kv": intra_kv, "intra_out": intra_out, "intra_up": intra_up, "intra_down": intra_down, "inter_query": inter_query, "inter_kv": inter_kv, "inter_out": inter_out, "inter_up": inter_up, "inter_down": inter_down, "w_mask": w_mask}


def norm_rows(values):
    center = values - lax.optimization_barrier(jnp.mean(values, axis=-1, keepdims=True))
    spread = lax.optimization_barrier(jnp.mean(center * center, axis=-1, keepdims=True))
    return center * lax.rsqrt(spread + 1e-05)

def positions_table(count, width):
    place = jnp.arange(count, dtype=jnp.float32)[:, None]
    index = jnp.arange(width // 2, dtype=jnp.float32)[None, :]
    angle = place * jnp.exp(-math.log(10000.0) * 2.0 * index / width)
    return jnp.concatenate([jnp.sin(angle), jnp.cos(angle)], axis=1)

def matmul(rows, weight):
    shape = rows.shape
    flat = rows.reshape(-1, shape[-1])
    result = jnp.dot(flat, weight, preferred_element_type=jnp.float32)
    return result.reshape(shape[:-1] + (weight.shape[1],))

def attend_one(items):
    query_vectors, key_matrix_rows, value_matrix_rows = items
    score_scale = 1.0 / math.sqrt(query_vectors.shape[-1])
    logit_scores = jnp.einsum('aur,nur->uan', query_vectors.astype(jnp.float32), key_matrix_rows.astype(jnp.float32)) * score_scale
    logit_scores = logit_scores - lax.optimization_barrier(jnp.max(logit_scores, axis=-1, keepdims=True))
    softmax_weights = jnp.exp(logit_scores)
    softmax_weights = (softmax_weights / lax.optimization_barrier(jnp.sum(softmax_weights, axis=-1, keepdims=True))).astype(jnp.bfloat16)
    return jnp.einsum('xra,axu->rxu', softmax_weights.astype(jnp.float32), value_matrix_rows.astype(jnp.float32)).astype(jnp.bfloat16)

def layer(inputs, w_query, w_kv, w_out, w_up, w_down):
    batch, length, width = inputs.shape
    depth = width // HEADS
    normed = norm_rows(inputs.astype(jnp.float32)).astype(jnp.bfloat16)
    query_vectors = matmul(normed, w_query).astype(jnp.bfloat16).reshape(batch, length, HEADS, depth)
    pair = matmul(normed, w_kv).astype(jnp.bfloat16)
    key_matrix_rows = pair[..., :width].reshape(batch, length, HEADS, depth)
    value_matrix_rows = pair[..., width:].reshape(batch, length, HEADS, depth)
    mixed = lax.map(attend_one, (query_vectors, key_matrix_rows, value_matrix_rows)).reshape(batch, length, width)
    middle_value = (inputs.astype(jnp.float32) + matmul(mixed, w_out)).astype(jnp.bfloat16)
    second_operand = norm_rows(middle_value.astype(jnp.float32)).astype(jnp.bfloat16)
    hidden = jax.nn.relu(matmul(second_operand, w_up)).astype(jnp.bfloat16)
    return (middle_value.astype(jnp.float32) + matmul(hidden, w_down)).astype(jnp.bfloat16)

def encode(audio, w_enc):
    blocks = audio.reshape(-1, STRIDE)
    after = jnp.concatenate([blocks[1:], jnp.zeros((1, STRIDE), jnp.float32)], axis=0)
    frames = jnp.concatenate([blocks, after], axis=1)
    result = jnp.dot(frames, w_enc, precision=lax.Precision.HIGHEST, preferred_element_type=jnp.float32)
    return jax.nn.relu(result).astype(jnp.bfloat16)

def reference(audio, w_enc, intra_query, intra_kv, intra_out, intra_up, intra_down, inter_query, inter_kv, inter_out, inter_up, inter_down, w_mask):
    enc = encode(audio, w_enc)
    padded = jnp.concatenate([enc, jnp.zeros((HOP, N), jnp.bfloat16)], axis=0)
    spans = jnp.concatenate([padded[:FRAMES].reshape(SPANS, HOP, N), padded[HOP:].reshape(SPANS, HOP, N)], axis=1)
    start = (spans.astype(jnp.float32) + positions_table(K, N)[None]).astype(jnp.bfloat16)
    intra = layer(start, intra_query, intra_kv, intra_out, intra_up, intra_down)
    across = jnp.transpose(intra, (1, 0, 2))
    across = (across.astype(jnp.float32) + positions_table(SPANS, N)[None]).astype(jnp.bfloat16)
    inter = layer(across, inter_query, inter_kv, inter_out, inter_up, inter_down)
    inter = jnp.transpose(inter, (1, 0, 2))
    first = inter[:, :HOP]
    earlier = jnp.concatenate([jnp.zeros((1, HOP, N), jnp.bfloat16), inter[:-1, HOP:]], axis=0)
    summed = (first.astype(jnp.float32) + earlier.astype(jnp.float32)).reshape(FRAMES, N).astype(jnp.bfloat16)
    mask = jax.nn.relu(jnp.dot(summed, w_mask, preferred_element_type=jnp.float32))
    repeated = jnp.concatenate([enc] * SPK, axis=1).astype(jnp.float32)
    return (mask * repeated).astype(jnp.bfloat16)
```

```python
import functools
import math

import jax
import jax.numpy as jnp
import numpy as np
from jax import lax
from jax.experimental import pallas as pl
from jax.experimental.pallas import tpu as pltpu
from jax.sharding import PartitionSpec as P

HEADS = 8
K = 256
HOP = 128
STRIDE = 8
SPK = 2


def shifted_2(block, axis, distance):
    devices = range(lax.axis_size(axis))
    route = [(i - distance, i) for i in devices if i - distance in devices]
    return lax.ppermute(block, axis, route)


def norm_rows(values):
    center = values - jnp.mean(values, axis=-1, keepdims=True)
    spread = jnp.mean(center * center, axis=-1, keepdims=True)
    return center * lax.rsqrt(spread + 1e-05)


def positions_table(count, width):
    place = jnp.arange(count, dtype=jnp.float32)[:, None]
    index = jnp.arange(width // 2, dtype=jnp.float32)[None, :]
    angle = place * jnp.exp(-math.log(10000.0) * 2.0 * index / width)
    return jnp.concatenate([jnp.sin(angle), jnp.cos(angle)], axis=1)


def matmul(rows, weight):
    shape = rows.shape
    flat = rows.reshape(-1, shape[-1])
    result = jnp.dot(flat, weight, preferred_element_type=jnp.float32)
    return result.reshape(shape[:-1] + (weight.shape[1],))


def attend_block(items):
    query_vectors, key_matrix_rows, value_matrix_rows = items
    score_scale = 1.0 / math.sqrt(query_vectors.shape[-1])
    logit_scores = (
        jnp.einsum(
            "blhd,bmhd->bhlm", query_vectors, key_matrix_rows, preferred_element_type=jnp.float32
        )
        * score_scale
    )
    logit_scores = logit_scores - jnp.max(logit_scores, axis=-1, keepdims=True)
    softmax_weights = jnp.exp(logit_scores)
    softmax_weights = (softmax_weights / jnp.sum(softmax_weights, axis=-1, keepdims=True)).astype(
        jnp.bfloat16
    )
    return jnp.einsum(
        "bhlm,bmhd->blhd", softmax_weights, value_matrix_rows, preferred_element_type=jnp.float32
    ).astype(jnp.bfloat16)


def layer(inputs, w_query, w_kv, w_out, w_up, w_down):
    batch, length, width = inputs.shape
    depth = width // HEADS
    group = math.gcd(batch, max(1, 1024 // length))
    blocks = batch // group
    normed = norm_rows(inputs.astype(jnp.float32)).astype(jnp.bfloat16)
    query_vectors = (
        matmul(normed, w_query).astype(jnp.bfloat16).reshape(blocks, group, length, HEADS, depth)
    )
    pair = matmul(normed, w_kv).astype(jnp.bfloat16)
    key_matrix_rows = pair[..., :width].reshape(blocks, group, length, HEADS, depth)
    value_matrix_rows = pair[..., width:].reshape(blocks, group, length, HEADS, depth)
    mixed = lax.map(attend_block, (query_vectors, key_matrix_rows, value_matrix_rows)).reshape(
        batch, length, width
    )
    middle_value = (inputs.astype(jnp.float32) + matmul(mixed, w_out)).astype(jnp.bfloat16)
    second_operand = norm_rows(middle_value.astype(jnp.float32)).astype(jnp.bfloat16)
    hidden = jax.nn.relu(matmul(second_operand, w_up)).astype(jnp.bfloat16)
    return (middle_value.astype(jnp.float32) + matmul(hidden, w_down)).astype(jnp.bfloat16)


def encode_rows(samples, w_enc):
    blocks = samples.reshape(-1, STRIDE)
    frames = jnp.concatenate([blocks[:-1], blocks[1:]], axis=1)
    result = jnp.dot(
        frames, w_enc, precision=lax.Precision.HIGHEST, preferred_element_type=jnp.float32
    )
    return jax.nn.relu(result).astype(jnp.bfloat16)


def plain_body(
    audio,
    w_enc,
    intra_query,
    intra_kv,
    intra_out,
    intra_up,
    intra_down,
    inter_query,
    inter_kv,
    inter_out,
    inter_up,
    inter_down,
    w_mask,
):
    frame_count = audio.shape[0] // STRIDE
    width = w_enc.shape[1]
    local_spans = frame_count // HOP
    devices = lax.axis_size("span")
    extra = shifted_2(audio[: (HOP + 1) * STRIDE], "span", -1)
    padded = encode_rows(jnp.concatenate([audio, extra], axis=0), w_enc)
    enc = padded[:frame_count]
    spans = jnp.concatenate(
        [
            padded[:frame_count].reshape(local_spans, HOP, width),
            padded[HOP:].reshape(local_spans, HOP, width),
        ],
        axis=1,
    )
    start = (spans.astype(jnp.float32) + positions_table(K, width)[None]).astype(jnp.bfloat16)
    intra = layer(start, intra_query, intra_kv, intra_out, intra_up, intra_down)
    per_device = K // devices
    grouped = intra.reshape(local_spans, devices, per_device, width)
    gathered = lax.all_to_all(grouped, "span", split_axis=1, concat_axis=0, tiled=True)
    total = gathered.shape[0]
    plain = gathered[:, 0]
    shifted = (plain.astype(jnp.float32) + positions_table(total, width)[:, None, :]).astype(
        jnp.bfloat16
    )
    turned = jnp.transpose(shifted, (1, 0, 2))
    result = layer(turned, inter_query, inter_kv, inter_out, inter_up, inter_down)
    inter = jnp.transpose(result, (1, 0, 2))[:, None]
    back = lax.all_to_all(inter, "span", split_axis=0, concat_axis=1, tiled=True).reshape(
        local_spans, K, width
    )
    second_half = back[:, HOP:]
    carried = shifted_2(second_half[-1], "span", 1)
    earlier = jnp.concatenate([carried[None], second_half[:-1]], axis=0)
    summed = back[:, :HOP].astype(jnp.float32) + earlier.astype(jnp.float32)
    summed = summed.reshape(frame_count, width).astype(jnp.bfloat16)
    mask = jax.nn.relu(jnp.dot(summed, w_mask, preferred_element_type=jnp.float32))
    repeated = jnp.concatenate([enc] * SPK, axis=1).astype(jnp.float32)
    return (mask * repeated).astype(jnp.bfloat16)


LANES = 128
TILE = 16
MESH = pl.DeviceIdType.MESH


def position_values(count, width):
    place = np.arange(count, dtype=np.float64)[:, None]
    index = np.arange(width // 2, dtype=np.float64)[None, :]
    angle = place * np.exp(-math.log(10000.0) * 2.0 * index / width)
    return np.concatenate([np.sin(angle), np.cos(angle)], axis=1).astype(np.float32)


def dot(left, right):
    return jnp.dot(left, right, preferred_element_type=jnp.float32)


def round_rows(values):
    return values.astype(jnp.bfloat16).astype(jnp.float32)


def strided(ref, first, count, stride):
    picked = [ref[side, pl.ds(first, count, stride=stride), :] for side in range(ref.shape[0])]
    return jnp.concatenate(picked, axis=1)


def attend_rows(query, key, value, bias):
    rows, width = query.shape
    depth = width // HEADS
    owner = lax.broadcasted_iota(jnp.int32, (1, width), 1) // depth
    zero = jnp.zeros((), jnp.bfloat16)
    total = None
    for head in range(HEADS):
        mine = owner == head
        scores = lax.dot_general(
            jnp.where(mine, query, zero),
            key,
            (((1,), (1,)), ((), ())),
            preferred_element_type=jnp.float32,
        )
        if bias is not None:
            scores = scores + bias
        scores = scores - jnp.max(scores, axis=-1, keepdims=True)
        weights = jnp.exp2(scores * (math.log2(math.e) / math.sqrt(depth)))
        weights = weights * (1.0 / jnp.sum(weights, axis=-1, keepdims=True))
        part = dot(weights.astype(jnp.bfloat16), jnp.where(mine, value, zero))
        total = part if total is None else total + part
    return total.astype(jnp.bfloat16)


def layer_rows(rows, group, bias, w_query, w_kv, w_out, w_up, w_down):
    width = rows.shape[1]
    normed = norm_rows(rows).astype(jnp.bfloat16)
    query = dot(normed, w_query[...]).astype(jnp.bfloat16)
    pair = dot(normed, w_kv[...]).astype(jnp.bfloat16)
    mixed = [
        attend_rows(
            query[at : at + group],
            pair[at : at + group, :width],
            pair[at : at + group, width:],
            bias,
        )
        for at in range(0, rows.shape[0], group)
    ]
    mixed = mixed[0] if len(mixed) == 1 else jnp.concatenate(mixed, axis=0)
    middle = round_rows(rows + dot(mixed, w_out[...]))
    second = norm_rows(middle).astype(jnp.bfloat16)
    hidden = jnp.maximum(dot(second, w_up[...]), 0.0).astype(jnp.bfloat16)
    return middle + dot(hidden, w_down[...])


def separator_kernel(
    devices,
    group,
    audio,
    w_enc,
    table_span,
    table_across,
    bias,
    intra_query,
    intra_kv,
    intra_out,
    intra_up,
    intra_down,
    inter_query,
    inter_kv,
    inter_out,
    inter_up,
    inter_down,
    enc_ref,
    summed_ref,
    samples,
    frames,
    sent,
    taken,
    across,
    inter,
    back,
    got,
    halo_send,
    halo_recv,
    out_send,
    out_recv,
    back_send,
    back_recv,
):
    me = lax.axis_index("span")
    width = w_enc.shape[1]
    rows = audio.shape[0]
    per_row = LANES // STRIDE
    count = rows * per_row
    spans = count // HOP
    share = HOP // devices
    total = spans * devices
    chunks = back.shape[0]
    part = share // chunks
    halo_rows = samples.shape[0] - rows

    barrier = pltpu.get_barrier_semaphore()
    for step in range(1, devices):
        other = lax.rem(me + step, devices)
        pl.semaphore_signal(barrier, inc=1, device_id={"span": other}, device_id_type=MESH)
    samples[:rows] = audio[...]
    pl.semaphore_wait(barrier, devices - 1)

    halo = pltpu.make_async_remote_copy(
        src_ref=audio.at[pl.ds(0, halo_rows)],
        dst_ref=samples.at[pl.ds(rows, halo_rows)],
        send_sem=halo_send,
        recv_sem=halo_recv,
        device_id={"span": lax.rem(me + devices - 1, devices)},
        device_id_type=MESH,
    )

    @pl.when(me > 0)
    def _():
        halo.start()

    lane = lax.broadcasted_iota(jnp.int32, (1, LANES), 1)
    slot = lax.broadcasted_iota(jnp.int32, (HOP, 1), 0) % per_row
    mine = lane // STRIDE == slot
    w_low = jnp.concatenate([w_enc[:STRIDE]] * per_row, axis=0)
    w_high = jnp.concatenate([w_enc[STRIDE:]] * per_row, axis=0)
    w_both = jnp.concatenate([w_low, w_high], axis=0)
    step_rows = HOP // per_row

    def encode(hop):
        at = hop * step_rows
        low = samples[pl.ds(at, step_rows), :]
        turned = pltpu.roll(samples[pl.ds(at, 2 * step_rows), :], LANES - STRIDE, 1)
        high = jnp.where(lane < LANES - STRIDE, turned[:step_rows], turned[1 : step_rows + 1])
        spread = [
            jnp.concatenate(
                [jnp.broadcast_to(block[r : r + 1], (per_row, LANES)) for r in range(step_rows)],
                axis=0,
            )
            for block in (low, high)
        ]
        picked = jnp.concatenate([jnp.where(mine, block, 0.0) for block in spread], axis=1)
        result = jnp.dot(
            picked, w_both, precision=lax.Precision.HIGHEST, preferred_element_type=jnp.float32
        )
        frames[pl.ds(hop * HOP, HOP), :] = jnp.maximum(result, 0.0).astype(jnp.bfloat16)

    for hop in range(spans - 1):
        encode(hop)

    def send_out(index, step):
        other = lax.rem(me + step, devices)
        return pltpu.make_async_remote_copy(
            src_ref=sent.at[index, :, pl.ds(pl.multiple_of(other * share, TILE), share), :],
            dst_ref=taken.at[me * spans + index],
            send_sem=out_send.at[index, step],
            recv_sem=out_recv.at[index, step],
            device_id={"span": other},
            device_id_type=MESH,
        )

    def do_span(index, _):
        @pl.when(index == spans - 2)
        def _():
            @pl.when(me < devices - 1)
            def _():
                halo.wait_recv()

            @pl.when(me == devices - 1)
            def _():
                samples[rows:] = jnp.zeros((halo_rows, LANES), jnp.float32)

            encode(spans - 1)
            encode(spans)

        at = pl.multiple_of(index * HOP, HOP)
        start = round_rows(
            frames[pl.ds(at, K), :].astype(jnp.float32) + table_span[...]
        )
        result = layer_rows(
            start, K, None, intra_query, intra_kv, intra_out, intra_up, intra_down
        ).astype(jnp.bfloat16)
        sent[index] = result.reshape(K // HOP, HOP, width)
        for step in range(1, devices):
            send_out(index, step).start()
        taken[me * spans + index] = sent[
            index, :, pl.ds(pl.multiple_of(me * share, TILE), share), :
        ]
        return 0

    lax.fori_loop(0, spans, do_span, 0)
    enc_ref[...] = frames[:count]

    owned = 2 * share

    def place(index, source):
        row = source * spans + index
        block = taken[row].reshape(owned, width).astype(jnp.float32)
        at = pl.multiple_of(row * owned, owned)
        block = round_rows(block + table_across[pl.ds(row, 1), :])
        for side in range(width // LANES):
            across[side, pl.ds(at, owned), :] = block[:, side * LANES : (side + 1) * LANES]

    def place_all(index, _):
        place(index, me)
        for step in range(1, devices):
            send_out(index, step).wait_recv()
            place(index, lax.rem(me + devices - step, devices))
        return 0

    lax.fori_loop(0, spans, place_all, 0)

    def send_back(chunk, step):
        other = lax.rem(me + step, devices)
        size = spans * part
        return pltpu.make_async_remote_copy(
            src_ref=back.at[chunk, pl.ds(pl.multiple_of(other * size, TILE), size), :],
            dst_ref=got.at[chunk, me],
            send_sem=back_send.at[chunk, step],
            recv_sem=back_recv.at[chunk, step],
            device_id={"span": other},
            device_id_type=MESH,
        )

    def do_chunk(chunk, _):
        def do_half(half, _):
            first = half * share + chunk * part
            block = jnp.concatenate(
                [strided(across, first + p, total, owned) for p in range(part)], axis=0
            )
            result = layer_rows(
                block, group, bias[...], inter_query, inter_kv, inter_out, inter_up, inter_down
            )
            at = pl.multiple_of(first * total, part * total)
            result = round_rows(result)
            for side in range(width // LANES):
                inter[side, pl.ds(at, part * total), :] = result[
                    :, side * LANES : (side + 1) * LANES
                ]
            return 0

        lax.fori_loop(0, 2, do_half, 0)
        near = chunk * part * total
        far = (share + chunk * part) * total
        pieces = []
        for span in range(total):
            piece = strided(inter, near + span, part, total)
            if span > 0:
                piece = piece + strided(inter, far + span - 1, part, total)
            pieces.append(piece)
        back[chunk] = jnp.concatenate(pieces, axis=0).astype(jnp.bfloat16)
        for step in range(1, devices):
            send_back(chunk, step).start()
        size = spans * part
        got[chunk, me] = back[chunk, pl.ds(pl.multiple_of(me * size, TILE), size), :]
        return 0

    lax.fori_loop(0, chunks, do_chunk, 0)

    def collect(source):
        pieces = [
            got[chunk, source].astype(jnp.float32).reshape(spans, part, width)
            for chunk in range(chunks)
        ]
        at = pl.multiple_of(source * share, TILE)
        summed_ref[:, pl.ds(at, share), :] = jnp.concatenate(pieces, axis=1).astype(jnp.bfloat16)

    collect(me)
    for step in range(1, devices):
        for chunk in range(chunks):
            send_back(chunk, step).wait_recv()
        collect(lax.rem(me + devices - step, devices))

    @pl.when(me > 0)
    def _():
        halo.wait_send()

    def drain_out(index, _):
        for step in range(1, devices):
            send_out(index, step).wait_send()
        return 0

    def drain_back(chunk, _):
        for step in range(1, devices):
            send_back(chunk, step).wait_send()
        return 0

    lax.fori_loop(0, spans, drain_out, 0)
    lax.fori_loop(0, chunks, drain_back, 0)


def kernel_body(devices, audio, w_enc, *weights):
    *layers, w_mask = weights
    width = w_enc.shape[1]
    rows = audio.shape[0] // LANES
    count = audio.shape[0] // STRIDE
    spans = count // HOP
    total = spans * devices
    share = HOP // devices
    chunks = 2
    part = share // chunks
    group = LANES
    halo_rows = 2 * HOP * STRIDE // LANES
    kind = np.arange(group) // total
    bias = np.where(kind[:, None] == kind[None, :], 0.0, -1e30).astype(np.float32)
    operands = (
        audio.reshape(rows, LANES),
        w_enc,
        position_values(K, width),
        position_values(total, width),
        bias,
        *layers,
    )
    vmem = pl.BlockSpec(memory_space=pltpu.VMEM)
    dma = pltpu.SemaphoreType.DMA
    enc, summed = pl.pallas_call(
        functools.partial(separator_kernel, devices, group),
        out_shape=[
            jax.ShapeDtypeStruct((count, width), jnp.bfloat16),
            jax.ShapeDtypeStruct((spans, HOP, width), jnp.bfloat16),
        ],
        in_specs=[vmem] * len(operands),
        out_specs=[vmem] * 2,
        scratch_shapes=[
            pltpu.VMEM((rows + halo_rows, LANES), jnp.float32),
            pltpu.VMEM((count + HOP, width), jnp.bfloat16),
            pltpu.VMEM((spans, K // HOP, HOP, width), jnp.bfloat16),
            pltpu.VMEM((total, K // HOP, share, width), jnp.bfloat16),
            pltpu.VMEM((width // LANES, total * 2 * share, LANES), jnp.float32),
            pltpu.VMEM((width // LANES, total * 2 * share, LANES), jnp.float32),
            pltpu.VMEM((chunks, total * part, width), jnp.bfloat16),
            pltpu.VMEM((chunks, devices, spans * part, width), jnp.bfloat16),
            dma,
            dma,
            dma((spans, devices)),
            dma((spans, devices)),
            dma((chunks, devices)),
            dma((chunks, devices)),
        ],
        compiler_params=pltpu.CompilerParams(
            collective_id=0, has_side_effects=True, vmem_limit_bytes=40 * 2**20
        ),
    )(*operands)
    summed = summed.reshape(count, width)
    mask = jax.nn.relu(jnp.dot(summed, w_mask, preferred_element_type=jnp.float32))
    repeated = jnp.concatenate([enc] * SPK, axis=1).astype(jnp.float32)
    return (mask * repeated).astype(jnp.bfloat16)


def fits_kernel(devices, count):
    spans = count // HOP
    share = HOP // devices
    return (
        HOP % devices == 0
        and share % TILE == 0
        and LANES % (spans * devices) == 0
        and spans >= 3
        and devices > 1
    )


def body(audio, w_enc, *weights):
    devices = lax.axis_size("span")
    if fits_kernel(devices, audio.shape[0] // STRIDE):
        return kernel_body(devices, audio, w_enc, *weights)
    return plain_body(audio, w_enc, *weights)


def solution(mesh):
    placed = (P(("mix", "span")), P(), P(), P(), P(), P(), P(), P(), P(), P(), P(), P(), P())
    return jax.shard_map(
        body, mesh=mesh, in_specs=placed, out_specs=P(("mix", "span"), None), check_vma=False
    )
```

```python
import functools
import math

import jax
import jax.numpy as jnp
import numpy as np
from jax import lax
from jax.experimental import pallas as pl
from jax.experimental.pallas import tpu as pltpu
from jax.sharding import PartitionSpec as P

HEADS = 8
K = 256
HOP = 128
STRIDE = 8
SPK = 2


def shifted_2(block, axis, distance):
    devices = range(lax.axis_size(axis))
    route = [(i - distance, i) for i in devices if i - distance in devices]
    return lax.ppermute(block, axis, route)


def norm_rows(values):
    center = values - jnp.mean(values, axis=-1, keepdims=True)
    spread = jnp.mean(center * center, axis=-1, keepdims=True)
    return center * lax.rsqrt(spread + 1e-05)


def positions_table(count, width):
    place = jnp.arange(count, dtype=jnp.float32)[:, None]
    index = jnp.arange(width // 2, dtype=jnp.float32)[None, :]
    angle = place * jnp.exp(-math.log(10000.0) * 2.0 * index / width)
    return jnp.concatenate([jnp.sin(angle), jnp.cos(angle)], axis=1)


def matmul(rows, weight):
    shape = rows.shape
    flat = rows.reshape(-1, shape[-1])
    result = jnp.dot(flat, weight, preferred_element_type=jnp.float32)
    return result.reshape(shape[:-1] + (weight.shape[1],))


def attend_block(items):
    query_vectors, key_matrix_rows, value_matrix_rows = items
    score_scale = 1.0 / math.sqrt(query_vectors.shape[-1])
    logit_scores = (
        jnp.einsum(
            "blhd,bmhd->bhlm", query_vectors, key_matrix_rows, preferred_element_type=jnp.float32
        )
        * score_scale
    )
    logit_scores = logit_scores - jnp.max(logit_scores, axis=-1, keepdims=True)
    softmax_weights = jnp.exp(logit_scores)
    softmax_weights = (softmax_weights / jnp.sum(softmax_weights, axis=-1, keepdims=True)).astype(
        jnp.bfloat16
    )
    return jnp.einsum(
        "bhlm,bmhd->blhd", softmax_weights, value_matrix_rows, preferred_element_type=jnp.float32
    ).astype(jnp.bfloat16)


def layer(inputs, w_query, w_kv, w_out, w_up, w_down):
    batch, length, width = inputs.shape
    depth = width // HEADS
    group = math.gcd(batch, max(1, 1024 // length))
    blocks = batch // group
    normed = norm_rows(inputs.astype(jnp.float32)).astype(jnp.bfloat16)
    query_vectors = (
        matmul(normed, w_query).astype(jnp.bfloat16).reshape(blocks, group, length, HEADS, depth)
    )
    pair = matmul(normed, w_kv).astype(jnp.bfloat16)
    key_matrix_rows = pair[..., :width].reshape(blocks, group, length, HEADS, depth)
    value_matrix_rows = pair[..., width:].reshape(blocks, group, length, HEADS, depth)
    mixed = lax.map(attend_block, (query_vectors, key_matrix_rows, value_matrix_rows)).reshape(
        batch, length, width
    )
    middle_value = (inputs.astype(jnp.float32) + matmul(mixed, w_out)).astype(jnp.bfloat16)
    second_operand = norm_rows(middle_value.astype(jnp.float32)).astype(jnp.bfloat16)
    hidden = jax.nn.relu(matmul(second_operand, w_up)).astype(jnp.bfloat16)
    return (middle_value.astype(jnp.float32) + matmul(hidden, w_down)).astype(jnp.bfloat16)


def encode_rows(samples, w_enc):
    blocks = samples.reshape(-1, STRIDE)
    frames = jnp.concatenate([blocks[:-1], blocks[1:]], axis=1)
    result = jnp.dot(
        frames, w_enc, precision=lax.Precision.HIGHEST, preferred_element_type=jnp.float32
    )
    return jax.nn.relu(result).astype(jnp.bfloat16)


def plain_body(
    audio,
    w_enc,
    intra_query,
    intra_kv,
    intra_out,
    intra_up,
    intra_down,
    inter_query,
    inter_kv,
    inter_out,
    inter_up,
    inter_down,
    w_mask,
):
    frame_count = audio.shape[0] // STRIDE
    width = w_enc.shape[1]
    local_spans = frame_count // HOP
    devices = lax.axis_size("span")
    extra = shifted_2(audio[: (HOP + 1) * STRIDE], "span", -1)
    padded = encode_rows(jnp.concatenate([audio, extra], axis=0), w_enc)
    enc = padded[:frame_count]
    spans = jnp.concatenate(
        [
            padded[:frame_count].reshape(local_spans, HOP, width),
            padded[HOP:].reshape(local_spans, HOP, width),
        ],
        axis=1,
    )
    start = (spans.astype(jnp.float32) + positions_table(K, width)[None]).astype(jnp.bfloat16)
    intra = layer(start, intra_query, intra_kv, intra_out, intra_up, intra_down)
    per_device = K // devices
    grouped = intra.reshape(local_spans, devices, per_device, width)
    gathered = lax.all_to_all(grouped, "span", split_axis=1, concat_axis=0, tiled=True)
    total = gathered.shape[0]
    plain = gathered[:, 0]
    shifted = (plain.astype(jnp.float32) + positions_table(total, width)[:, None, :]).astype(
        jnp.bfloat16
    )
    turned = jnp.transpose(shifted, (1, 0, 2))
    result = layer(turned, inter_query, inter_kv, inter_out, inter_up, inter_down)
    inter = jnp.transpose(result, (1, 0, 2))[:, None]
    back = lax.all_to_all(inter, "span", split_axis=0, concat_axis=1, tiled=True).reshape(
        local_spans, K, width
    )
    second_half = back[:, HOP:]
    carried = shifted_2(second_half[-1], "span", 1)
    earlier = jnp.concatenate([carried[None], second_half[:-1]], axis=0)
    summed = back[:, :HOP].astype(jnp.float32) + earlier.astype(jnp.float32)
    summed = summed.reshape(frame_count, width).astype(jnp.bfloat16)
    mask = jax.nn.relu(jnp.dot(summed, w_mask, preferred_element_type=jnp.float32))
    repeated = jnp.concatenate([enc] * SPK, axis=1).astype(jnp.float32)
    return (mask * repeated).astype(jnp.bfloat16)


LANES = 128
TILE = 16
OPERANDS = 14
MESH = pl.DeviceIdType.MESH


def position_values(count, width):
    place = np.arange(count, dtype=np.float64)[:, None]
    index = np.arange(width // 2, dtype=np.float64)[None, :]
    angle = place * np.exp(-math.log(10000.0) * 2.0 * index / width)
    return np.concatenate([np.sin(angle), np.cos(angle)], axis=1).astype(np.float32)


def dot(left, right):
    return jnp.dot(left, right, preferred_element_type=jnp.float32)


def round_rows(values):
    return values.astype(jnp.bfloat16).astype(jnp.float32)


def strided(ref, first, count, stride):
    picked = [ref[side, pl.ds(first, count, stride=stride), :] for side in range(ref.shape[0])]
    return jnp.concatenate(picked, axis=1)


def attend_rows(query, key, value, bias):
    rows, width = query.shape
    depth = width // HEADS
    owner = lax.broadcasted_iota(jnp.int32, (1, LANES), 1) // depth
    zero = jnp.zeros((), jnp.bfloat16)
    ones = jnp.ones((rows, LANES), jnp.bfloat16)
    heads = LANES // depth
    sides = []
    for at in range(0, width, LANES):
        side_query, side_key, side_value = (
            block[:, at : at + LANES] for block in (query, key, value)
        )
        scores = lax.dot_general(
            jnp.concatenate(
                [jnp.where(owner == head, side_query, zero) for head in range(heads)], axis=0
            ),
            side_key,
            (((1,), (1,)), ((), ())),
            preferred_element_type=jnp.float32,
        )
        weights = []
        values = []
        for head in range(heads):
            part = scores[head * rows : (head + 1) * rows]
            if bias is not None:
                part = part + bias
            part = part - jnp.max(part, axis=-1, keepdims=True)
            weights.append(jnp.exp2(part.astype(jnp.bfloat16)))
            mine = owner == head
            values.append(
                jnp.concatenate(
                    [jnp.where(mine, side_value, zero), jnp.where(mine, ones, zero)], axis=1
                )
            )
        result = dot(jnp.concatenate(weights, axis=1), jnp.concatenate(values, axis=0))
        sides.append(result[:, :LANES] / result[:, LANES:])
    return jnp.concatenate(sides, axis=1).astype(jnp.bfloat16)


def layer_rows(rows, group, bias, w_query, w_kv, w_out, w_up, w_down):
    width = rows.shape[1]
    normed = norm_rows(rows).astype(jnp.bfloat16)
    scale = math.log2(math.e) / math.sqrt(width // HEADS)
    query = (dot(normed, w_query[...]) * scale).astype(jnp.bfloat16)
    pair = dot(normed, w_kv[...]).astype(jnp.bfloat16)
    mixed = [
        attend_rows(
            query[at : at + group],
            pair[at : at + group, :width],
            pair[at : at + group, width:],
            bias,
        )
        for at in range(0, rows.shape[0], group)
    ]
    mixed = mixed[0] if len(mixed) == 1 else jnp.concatenate(mixed, axis=0)
    middle = round_rows(rows + dot(mixed, w_out[...]))
    second = norm_rows(middle).astype(jnp.bfloat16)
    hidden = jnp.maximum(dot(second, w_up[...]), 0.0).astype(jnp.bfloat16)
    return middle + dot(hidden, w_down[...])


def separator_kernel(
    devices,
    group,
    *refs,
):
    given, refs = refs[:OPERANDS], refs[OPERANDS:]
    (enc_ref, summed_ref), refs = refs[:2], refs[2:]
    held, refs = refs[:OPERANDS], refs[OPERANDS:]
    audio = given[0]
    samples, w_enc, table_span, table_across, *layers = held
    intra, inter_weights = layers[:5], layers[5:]
    (
    frames,
    sent,
    taken,
    across,
    inter,
    back,
    got,
    halo_send,
    halo_recv,
    out_send,
    out_recv,
    back_send,
    back_recv,
    load,
    ) = refs
    me = lax.axis_index("span")
    width = w_enc.shape[1]
    rows = audio.shape[0]
    per_row = LANES // STRIDE
    count = rows * per_row
    spans = count // HOP
    share = HOP // devices
    total = spans * devices
    chunks = back.shape[0]
    part = share // chunks
    halo_rows = samples.shape[0] - rows

    loads = []
    for index in range(OPERANDS):
        target = samples.at[pl.ds(0, rows)] if index == 0 else held[index]
        loads.append(pltpu.make_async_copy(given[index], target, load.at[index]))
        loads[-1].start()

    barrier = pltpu.get_barrier_semaphore()
    for step in range(1, devices):
        other = lax.rem(me + step, devices)
        pl.semaphore_signal(barrier, inc=1, device_id={"span": other}, device_id_type=MESH)
    pl.semaphore_wait(barrier, devices - 1)

    halo = pltpu.make_async_remote_copy(
        src_ref=audio.at[pl.ds(0, halo_rows)],
        dst_ref=samples.at[pl.ds(rows, halo_rows)],
        send_sem=halo_send,
        recv_sem=halo_recv,
        device_id={"span": lax.rem(me + devices - 1, devices)},
        device_id_type=MESH,
    )

    @pl.when(me > 0)
    def _():
        halo.start()

    lane = lax.broadcasted_iota(jnp.int32, (1, LANES), 1)
    slot = lax.broadcasted_iota(jnp.int32, (HOP, 1), 0) % per_row
    mine = lane // STRIDE == slot
    for index in range(4):
        loads[index].wait()
    w_low = jnp.concatenate([w_enc[:STRIDE]] * per_row, axis=0)
    w_high = jnp.concatenate([w_enc[STRIDE:]] * per_row, axis=0)
    w_both = jnp.concatenate([w_low, w_high], axis=0)
    step_rows = HOP // per_row

    kind = [lax.broadcasted_iota(jnp.int32, (group, group), axis) // total for axis in (0, 1)]
    bias = jnp.where(kind[0] == kind[1], 0.0, -1e30)

    def encode(hop):
        at = hop * step_rows
        low = samples[pl.ds(at, step_rows), :]
        turned = pltpu.roll(samples[pl.ds(at, 2 * step_rows), :], LANES - STRIDE, 1)
        high = jnp.where(lane < LANES - STRIDE, turned[:step_rows], turned[1 : step_rows + 1])
        spread = [
            jnp.concatenate(
                [jnp.broadcast_to(block[r : r + 1], (per_row, LANES)) for r in range(step_rows)],
                axis=0,
            )
            for block in (low, high)
        ]
        picked = jnp.concatenate([jnp.where(mine, block, 0.0) for block in spread], axis=1)
        result = jnp.dot(
            picked, w_both, precision=lax.Precision.HIGHEST, preferred_element_type=jnp.float32
        )
        frames[pl.ds(hop * HOP, HOP), :] = jnp.maximum(result, 0.0).astype(jnp.bfloat16)

    for hop in range(spans - 1):
        encode(hop)

    for index in range(4, 9):
        loads[index].wait()

    def send_out(index, step):
        other = lax.rem(me + step, devices)
        return pltpu.make_async_remote_copy(
            src_ref=sent.at[index, :, pl.ds(pl.multiple_of(other * share, TILE), share), :],
            dst_ref=taken.at[me * spans + index],
            send_sem=out_send.at[index, step],
            recv_sem=out_recv.at[index, step],
            device_id={"span": other},
            device_id_type=MESH,
        )

    def do_spans(pair, _):
        @pl.when(pair == spans // 2 - 1)
        def _():
            @pl.when(me < devices - 1)
            def _():
                halo.wait_recv()

            @pl.when(me == devices - 1)
            def _():
                samples[rows:] = jnp.zeros((halo_rows, LANES), jnp.float32)

            encode(spans - 1)
            encode(spans)

        starts = []
        for side in range(2):
            at = pl.multiple_of((2 * pair + side) * HOP, HOP)
            starts.append(
                round_rows(frames[pl.ds(at, K), :].astype(jnp.float32) + table_span[...])
            )
        result = layer_rows(jnp.concatenate(starts, axis=0), K, None, *intra)
        result = result.astype(jnp.bfloat16)
        for side in range(2):
            index = 2 * pair + side
            sent[index] = result[side * K : (side + 1) * K].reshape(K // HOP, HOP, width)
            for step in range(1, devices):
                send_out(index, step).start()
            taken[me * spans + index] = sent[
                index, :, pl.ds(pl.multiple_of(me * share, TILE), share), :
            ]
        return 0

    lax.fori_loop(0, spans // 2, do_spans, 0)
    enc_ref[...] = frames[:count]

    for index in range(9, OPERANDS):
        loads[index].wait()
    owned = 2 * share

    def place(index, source):
        row = source * spans + index
        block = taken[row].reshape(owned, width).astype(jnp.float32)
        at = pl.multiple_of(row * owned, owned)
        block = round_rows(block + table_across[pl.ds(row, 1), :])
        for side in range(width // LANES):
            across[side, pl.ds(at, owned), :] = block[:, side * LANES : (side + 1) * LANES]

    def place_all(index, _):
        place(index, me)
        for step in range(1, devices):
            send_out(index, step).wait_recv()
            place(index, lax.rem(me + devices - step, devices))
        return 0

    lax.fori_loop(0, spans, place_all, 0)

    def send_back(chunk, step):
        other = lax.rem(me + step, devices)
        size = spans * part
        return pltpu.make_async_remote_copy(
            src_ref=back.at[chunk, pl.ds(pl.multiple_of(other * size, TILE), size), :],
            dst_ref=got.at[chunk, me],
            send_sem=back_send.at[chunk, step],
            recv_sem=back_recv.at[chunk, step],
            device_id={"span": other},
            device_id_type=MESH,
        )

    def do_chunk(chunk, _):
        firsts = [half * share + chunk * part for half in range(2)]
        block = jnp.concatenate(
            [strided(across, first + p, total, owned) for first in firsts for p in range(part)],
            axis=0,
        )
        result = round_rows(layer_rows(block, group, bias, *inter_weights))
        size = part * total
        for half, first in enumerate(firsts):
            at = pl.multiple_of(first * total, size)
            for side in range(width // LANES):
                inter[side, pl.ds(at, size), :] = result[
                    half * size : (half + 1) * size, side * LANES : (side + 1) * LANES
                ]
        near = chunk * part * total
        far = (share + chunk * part) * total
        pieces = []
        for span in range(total):
            piece = strided(inter, near + span, part, total)
            if span > 0:
                piece = piece + strided(inter, far + span - 1, part, total)
            pieces.append(piece)
        back[chunk] = jnp.concatenate(pieces, axis=0).astype(jnp.bfloat16)
        for step in range(1, devices):
            send_back(chunk, step).start()
        size = spans * part
        got[chunk, me] = back[chunk, pl.ds(pl.multiple_of(me * size, TILE), size), :]
        return 0

    lax.fori_loop(0, chunks, do_chunk, 0)

    def collect(source):
        pieces = [
            got[chunk, source].astype(jnp.float32).reshape(spans, part, width)
            for chunk in range(chunks)
        ]
        at = pl.multiple_of(source * share, TILE)
        summed_ref[:, pl.ds(at, share), :] = jnp.concatenate(pieces, axis=1).astype(jnp.bfloat16)

    collect(me)
    for step in range(1, devices):
        for chunk in range(chunks):
            send_back(chunk, step).wait_recv()
        collect(lax.rem(me + devices - step, devices))

    @pl.when(me > 0)
    def _():
        halo.wait_send()

    def drain_out(index, _):
        for step in range(1, devices):
            send_out(index, step).wait_send()
        return 0

    def drain_back(chunk, _):
        for step in range(1, devices):
            send_back(chunk, step).wait_send()
        return 0

    lax.fori_loop(0, spans, drain_out, 0)
    lax.fori_loop(0, chunks, drain_back, 0)


def kernel_body(devices, audio, w_enc, *weights):
    *layers, w_mask = weights
    width = w_enc.shape[1]
    rows = audio.shape[0] // LANES
    count = audio.shape[0] // STRIDE
    spans = count // HOP
    total = spans * devices
    share = HOP // devices
    chunks = 2
    part = share // chunks
    group = LANES
    halo_rows = 2 * HOP * STRIDE // LANES
    operands = (
        audio.reshape(rows, LANES),
        w_enc,
        position_values(K, width),
        position_values(total, width),
        *layers,
    )
    vmem = pl.BlockSpec(memory_space=pltpu.VMEM)
    far = pl.BlockSpec(memory_space=pl.ANY)
    dma = pltpu.SemaphoreType.DMA
    enc, summed = pl.pallas_call(
        functools.partial(separator_kernel, devices, group),
        out_shape=[
            jax.ShapeDtypeStruct((count, width), jnp.bfloat16),
            jax.ShapeDtypeStruct((spans, HOP, width), jnp.bfloat16),
        ],
        in_specs=[far] * len(operands),
        out_specs=[vmem] * 2,
        scratch_shapes=[
            pltpu.VMEM((rows + halo_rows, LANES), jnp.float32),
            *[pltpu.VMEM(operand.shape, operand.dtype) for operand in operands[1:]],
            pltpu.VMEM((count + HOP, width), jnp.bfloat16),
            pltpu.VMEM((spans, K // HOP, HOP, width), jnp.bfloat16),
            pltpu.VMEM((total, K // HOP, share, width), jnp.bfloat16),
            pltpu.VMEM((width // LANES, total * 2 * share, LANES), jnp.float32),
            pltpu.VMEM((width // LANES, total * 2 * share, LANES), jnp.float32),
            pltpu.VMEM((chunks, total * part, width), jnp.bfloat16),
            pltpu.VMEM((chunks, devices, spans * part, width), jnp.bfloat16),
            dma,
            dma,
            dma((spans, devices)),
            dma((spans, devices)),
            dma((chunks, devices)),
            dma((chunks, devices)),
            dma((len(operands),)),
        ],
        compiler_params=pltpu.CompilerParams(
            collective_id=0, has_side_effects=True, vmem_limit_bytes=60 * 2**20
        ),
    )(*operands)
    summed = summed.reshape(count, width)
    mask = jax.nn.relu(jnp.dot(summed, w_mask, preferred_element_type=jnp.float32))
    repeated = jnp.concatenate([enc] * SPK, axis=1).astype(jnp.float32)
    return (mask * repeated).astype(jnp.bfloat16)


def fits_kernel(devices, count):
    spans = count // HOP
    share = HOP // devices
    return (
        HOP % devices == 0
        and share % TILE == 0
        and LANES % (spans * devices) == 0
        and spans >= 4
        and spans % 2 == 0
        and devices > 1
    )


def body(audio, w_enc, *weights):
    devices = lax.axis_size("span")
    if fits_kernel(devices, audio.shape[0] // STRIDE):
        return kernel_body(devices, audio, w_enc, *weights)
    return plain_body(audio, w_enc, *weights)


def solution(mesh):
    placed = (P(("mix", "span")), P(), P(), P(), P(), P(), P(), P(), P(), P(), P(), P(), P())
    return jax.shard_map(
        body, mesh=mesh, in_specs=placed, out_specs=P(("mix", "span"), None), check_vma=False
    )
```

```python
import functools
import math

import jax
import jax.numpy as jnp
import numpy as np
from jax import lax
from jax.experimental import pallas as pl
from jax.experimental.pallas import tpu as pltpu
from jax.sharding import PartitionSpec as P

HEADS = 8
K = 256
HOP = 128
STRIDE = 8
SPK = 2


def shifted_2(block, axis, distance):
    devices = range(lax.axis_size(axis))
    route = [(i - distance, i) for i in devices if i - distance in devices]
    return lax.ppermute(block, axis, route)


def norm_rows(values):
    center = values - jnp.mean(values, axis=-1, keepdims=True)
    spread = jnp.mean(center * center, axis=-1, keepdims=True)
    return center * lax.rsqrt(spread + 1e-05)


def positions_table(count, width):
    place = jnp.arange(count, dtype=jnp.float32)[:, None]
    index = jnp.arange(width // 2, dtype=jnp.float32)[None, :]
    angle = place * jnp.exp(-math.log(10000.0) * 2.0 * index / width)
    return jnp.concatenate([jnp.sin(angle), jnp.cos(angle)], axis=1)


def matmul(rows, weight):
    shape = rows.shape
    flat = rows.reshape(-1, shape[-1])
    result = jnp.dot(flat, weight, preferred_element_type=jnp.float32)
    return result.reshape(shape[:-1] + (weight.shape[1],))


def attend_block(items):
    query_vectors, key_matrix_rows, value_matrix_rows = items
    score_scale = 1.0 / math.sqrt(query_vectors.shape[-1])
    logit_scores = (
        jnp.einsum(
            "blhd,bmhd->bhlm", query_vectors, key_matrix_rows, preferred_element_type=jnp.float32
        )
        * score_scale
    )
    logit_scores = logit_scores - jnp.max(logit_scores, axis=-1, keepdims=True)
    softmax_weights = jnp.exp(logit_scores)
    softmax_weights = (softmax_weights / jnp.sum(softmax_weights, axis=-1, keepdims=True)).astype(
        jnp.bfloat16
    )
    return jnp.einsum(
        "bhlm,bmhd->blhd", softmax_weights, value_matrix_rows, preferred_element_type=jnp.float32
    ).astype(jnp.bfloat16)


def layer(inputs, w_query, w_kv, w_out, w_up, w_down):
    batch, length, width = inputs.shape
    depth = width // HEADS
    group = math.gcd(batch, max(1, 1024 // length))
    blocks = batch // group
    normed = norm_rows(inputs.astype(jnp.float32)).astype(jnp.bfloat16)
    query_vectors = (
        matmul(normed, w_query).astype(jnp.bfloat16).reshape(blocks, group, length, HEADS, depth)
    )
    pair = matmul(normed, w_kv).astype(jnp.bfloat16)
    key_matrix_rows = pair[..., :width].reshape(blocks, group, length, HEADS, depth)
    value_matrix_rows = pair[..., width:].reshape(blocks, group, length, HEADS, depth)
    mixed = lax.map(attend_block, (query_vectors, key_matrix_rows, value_matrix_rows)).reshape(
        batch, length, width
    )
    middle_value = (inputs.astype(jnp.float32) + matmul(mixed, w_out)).astype(jnp.bfloat16)
    second_operand = norm_rows(middle_value.astype(jnp.float32)).astype(jnp.bfloat16)
    hidden = jax.nn.relu(matmul(second_operand, w_up)).astype(jnp.bfloat16)
    return (middle_value.astype(jnp.float32) + matmul(hidden, w_down)).astype(jnp.bfloat16)


def encode_rows(samples, w_enc):
    blocks = samples.reshape(-1, STRIDE)
    frames = jnp.concatenate([blocks[:-1], blocks[1:]], axis=1)
    result = jnp.dot(
        frames, w_enc, precision=lax.Precision.HIGHEST, preferred_element_type=jnp.float32
    )
    return jax.nn.relu(result).astype(jnp.bfloat16)


def plain_body(
    audio,
    w_enc,
    intra_query,
    intra_kv,
    intra_out,
    intra_up,
    intra_down,
    inter_query,
    inter_kv,
    inter_out,
    inter_up,
    inter_down,
    w_mask,
):
    frame_count = audio.shape[0] // STRIDE
    width = w_enc.shape[1]
    local_spans = frame_count // HOP
    devices = lax.axis_size("span")
    extra = shifted_2(audio[: (HOP + 1) * STRIDE], "span", -1)
    padded = encode_rows(jnp.concatenate([audio, extra], axis=0), w_enc)
    enc = padded[:frame_count]
    spans = jnp.concatenate(
        [
            padded[:frame_count].reshape(local_spans, HOP, width),
            padded[HOP:].reshape(local_spans, HOP, width),
        ],
        axis=1,
    )
    start = (spans.astype(jnp.float32) + positions_table(K, width)[None]).astype(jnp.bfloat16)
    intra = layer(start, intra_query, intra_kv, intra_out, intra_up, intra_down)
    per_device = K // devices
    grouped = intra.reshape(local_spans, devices, per_device, width)
    gathered = lax.all_to_all(grouped, "span", split_axis=1, concat_axis=0, tiled=True)
    total = gathered.shape[0]
    plain = gathered[:, 0]
    shifted = (plain.astype(jnp.float32) + positions_table(total, width)[:, None, :]).astype(
        jnp.bfloat16
    )
    turned = jnp.transpose(shifted, (1, 0, 2))
    result = layer(turned, inter_query, inter_kv, inter_out, inter_up, inter_down)
    inter = jnp.transpose(result, (1, 0, 2))[:, None]
    back = lax.all_to_all(inter, "span", split_axis=0, concat_axis=1, tiled=True).reshape(
        local_spans, K, width
    )
    second_half = back[:, HOP:]
    carried = shifted_2(second_half[-1], "span", 1)
    earlier = jnp.concatenate([carried[None], second_half[:-1]], axis=0)
    summed = back[:, :HOP].astype(jnp.float32) + earlier.astype(jnp.float32)
    summed = summed.reshape(frame_count, width).astype(jnp.bfloat16)
    mask = jax.nn.relu(jnp.dot(summed, w_mask, preferred_element_type=jnp.float32))
    repeated = jnp.concatenate([enc] * SPK, axis=1).astype(jnp.float32)
    return (mask * repeated).astype(jnp.bfloat16)


LANES = 128
TILE = 16
OPERANDS = 14
MESH = pl.DeviceIdType.MESH


def position_values(count, width):
    place = np.arange(count, dtype=np.float64)[:, None]
    index = np.arange(width // 2, dtype=np.float64)[None, :]
    angle = place * np.exp(-math.log(10000.0) * 2.0 * index / width)
    return np.concatenate([np.sin(angle), np.cos(angle)], axis=1).astype(np.float32)


def dot(left, right):
    return jnp.dot(left, right, preferred_element_type=jnp.float32)


def round_rows(values):
    return values.astype(jnp.bfloat16).astype(jnp.float32)


def strided(ref, first, count, stride):
    picked = [ref[side, pl.ds(first, count, stride=stride), :] for side in range(ref.shape[0])]
    return jnp.concatenate(picked, axis=1)


def attend_rows(query, key, value, bias):
    rows, width = query.shape
    depth = width // HEADS
    owner = lax.broadcasted_iota(jnp.int32, (1, LANES), 1) // depth
    zero = jnp.zeros((), jnp.bfloat16)
    ones = jnp.ones((rows, LANES), jnp.bfloat16)
    heads = LANES // depth
    sides = []
    for at in range(0, width, LANES):
        side_query, side_key, side_value = (
            block[:, at : at + LANES] for block in (query, key, value)
        )
        scores = lax.dot_general(
            jnp.concatenate(
                [jnp.where(owner == head, side_query, zero) for head in range(heads)], axis=0
            ),
            side_key,
            (((1,), (1,)), ((), ())),
            preferred_element_type=jnp.float32,
        )
        weights = []
        values = []
        for head in range(heads):
            part = scores[head * rows : (head + 1) * rows]
            if bias is not None:
                part = part + bias
            part = part - jnp.max(part, axis=-1, keepdims=True)
            weights.append(jnp.exp2(part.astype(jnp.bfloat16)))
            mine = owner == head
            values.append(
                jnp.concatenate(
                    [jnp.where(mine, side_value, zero), jnp.where(mine, ones, zero)], axis=1
                )
            )
        result = dot(jnp.concatenate(weights, axis=1), jnp.concatenate(values, axis=0))
        sides.append(result[:, :LANES] / result[:, LANES:])
    return jnp.concatenate(sides, axis=1).astype(jnp.bfloat16)


def attend_few(query, key, value):
    rows, width = query.shape
    depth = width // HEADS
    owner = lax.broadcasted_iota(jnp.int32, (1, LANES), 1) // depth
    zero = jnp.zeros((), jnp.bfloat16)
    ones = jnp.ones((key.shape[0], LANES), jnp.bfloat16)
    heads = LANES // depth
    sides = []
    for at in range(0, width, LANES):
        side_query, side_key, side_value = (
            block[:, at : at + LANES] for block in (query, key, value)
        )
        scores = lax.dot_general(
            jnp.concatenate(
                [jnp.where(owner == head, side_query, zero) for head in range(heads)], axis=0
            ),
            side_key,
            (((1,), (1,)), ((), ())),
            preferred_element_type=jnp.float32,
        )
        scores = scores - jnp.max(scores, axis=-1, keepdims=True)
        weights = jnp.exp2(scores.astype(jnp.bfloat16))
        result = dot(weights, jnp.concatenate([side_value, ones], axis=1))
        result = result[:, :LANES] / result[:, LANES:]
        total = jnp.where(owner == 0, result[:rows], 0.0)
        for head in range(1, heads):
            total = jnp.where(owner == head, result[head * rows : (head + 1) * rows], total)
        sides.append(total)
    return jnp.concatenate(sides, axis=1).astype(jnp.bfloat16)


def query_rows(normed, w_query):
    scale = math.log2(math.e) / math.sqrt(normed.shape[1] // HEADS)
    return (dot(normed, w_query[...]) * scale).astype(jnp.bfloat16)


def rest_rows(rows, mixed, w_out, w_up, w_down):
    middle = round_rows(rows + dot(mixed, w_out[...]))
    second = norm_rows(middle).astype(jnp.bfloat16)
    hidden = jnp.maximum(dot(second, w_up[...]), 0.0).astype(jnp.bfloat16)
    return middle + dot(hidden, w_down[...])


def layer_rows(rows, group, bias, w_query, w_kv, w_out, w_up, w_down):
    width = rows.shape[1]
    normed = norm_rows(rows).astype(jnp.bfloat16)
    query = query_rows(normed, w_query)
    pair = dot(normed, w_kv[...]).astype(jnp.bfloat16)
    mixed = [
        attend_rows(
            query[at : at + group],
            pair[at : at + group, :width],
            pair[at : at + group, width:],
            bias,
        )
        for at in range(0, rows.shape[0], group)
    ]
    return rest_rows(rows, jnp.concatenate(mixed, axis=0), w_out, w_up, w_down)


def separator_kernel(devices, group, *refs):
    given, refs = refs[:OPERANDS], refs[OPERANDS:]
    (enc_ref, summed_ref), refs = refs[:2], refs[2:]
    held, refs = refs[:OPERANDS], refs[OPERANDS:]
    audio = given[0]
    samples, w_enc, table_span, table_across, *layers = held
    intra_query, intra_kv, *intra_rest = layers[:5]
    inter_weights = layers[5:]
    (
        frames,
        normed,
        started,
        mixed,
        across,
        inter,
        back,
        got,
        audio_send,
        audio_recv,
        back_send,
        back_recv,
        load,
    ) = refs
    me = lax.axis_index("span")
    width = w_enc.shape[1]
    rows = audio.shape[0]
    per_row = LANES // STRIDE
    count = rows * per_row
    spans = count // HOP
    share = HOP // devices
    owned = 2 * share
    total = spans * devices
    chunks = back.shape[0]
    part = share // chunks

    own_rows = samples.at[pl.ds(pl.multiple_of(me * rows, rows), rows)]
    loads = []
    for index in range(OPERANDS):
        target = own_rows if index == 0 else held[index]
        loads.append(pltpu.make_async_copy(given[index], target, load.at[index]))
        loads[-1].start()

    barrier = pltpu.get_barrier_semaphore()
    for step in range(1, devices):
        other = lax.rem(me + step, devices)
        pl.semaphore_signal(barrier, inc=1, device_id={"span": other}, device_id_type=MESH)
    ending = samples.shape[0] - rows * devices
    samples[rows * devices :] = jnp.zeros((ending, LANES), jnp.float32)
    pl.semaphore_wait(barrier, devices - 1)

    def send_audio(step):
        return pltpu.make_async_remote_copy(
            src_ref=audio,
            dst_ref=own_rows,
            send_sem=audio_send.at[step],
            recv_sem=audio_recv.at[step],
            device_id={"span": lax.rem(me + step, devices)},
            device_id_type=MESH,
        )

    for step in (devices - 1, *range(1, devices - 1)):
        send_audio(step).start()

    lane = lax.broadcasted_iota(jnp.int32, (1, LANES), 1)
    slot = lax.broadcasted_iota(jnp.int32, (HOP, 1), 0) % per_row
    mine = lane // STRIDE == slot
    for index in range(4):
        loads[index].wait()
    w_low = jnp.concatenate([w_enc[:STRIDE]] * per_row, axis=0)
    w_high = jnp.concatenate([w_enc[STRIDE:]] * per_row, axis=0)
    w_both = jnp.concatenate([w_low, w_high], axis=0)
    w_lead = w_both.astype(jnp.bfloat16)
    w_rest = (w_both - w_lead.astype(jnp.float32)).astype(jnp.bfloat16)
    step_rows = HOP // per_row
    kind = [lax.broadcasted_iota(jnp.int32, (group, group), axis) // total for axis in (0, 1)]
    bias = jnp.where(kind[0] == kind[1], 0.0, -1e30)

    def encode(hop):
        at = pl.multiple_of(hop * step_rows, step_rows)
        low = samples[pl.ds(at, step_rows), :]
        turned = pltpu.roll(samples[pl.ds(at, 2 * step_rows), :], LANES - STRIDE, 1)
        high = jnp.where(lane < LANES - STRIDE, turned[:step_rows], turned[1 : step_rows + 1])
        leads = []
        rests = []
        for block in (low, high):
            lead = block.astype(jnp.bfloat16).astype(jnp.float32)
            for values, into in ((lead, leads), (block - lead, rests)):
                spread = jnp.concatenate(
                    [
                        jnp.broadcast_to(values[r : r + 1], (per_row, LANES))
                        for r in range(step_rows)
                    ],
                    axis=0,
                )
                into.append(jnp.where(mine, spread, 0.0).astype(jnp.bfloat16))
        lead = jnp.concatenate(leads, axis=1)
        rest = jnp.concatenate(rests, axis=1)
        result = dot(lead, w_lead) + (dot(rest, w_lead) + dot(lead, w_rest))
        at = pl.multiple_of(hop * HOP, HOP)
        frames[pl.ds(at, HOP), :] = jnp.maximum(result, 0.0).astype(jnp.bfloat16)

    send_audio(devices - 1).wait_recv()
    encode((me + 1) * spans)
    for index in range(4, 9):
        loads[index].wait()
    own = pl.multiple_of(me * share, TILE)

    def attend_source(step, _):
        @pl.when((step > 0) & (step < devices - 1))
        def _():
            send_audio(step).wait_recv()

        source = lax.rem(me + devices - step, devices)
        for index in range(spans):
            encode(source * spans + index)
        for index in range(spans):
            span = source * spans + index
            at = pl.multiple_of(span * HOP, HOP)
            start = round_rows(frames[pl.ds(at, K), :].astype(jnp.float32) + table_span[...])
            values = norm_rows(start).astype(jnp.bfloat16)
            normed[index] = values.reshape(K // HOP, HOP, width)
            for half in range(K // HOP):
                at = pl.multiple_of(span * HOP + half * HOP + own, TILE)
                table = table_span[pl.ds(pl.multiple_of(half * HOP + own, TILE), share), :]
                value = round_rows(frames[pl.ds(at, share), :].astype(jnp.float32) + table)
                at = pl.multiple_of(span * owned + half * share, TILE)
                started[pl.ds(at, share), :] = value
        pair = dot(normed[...].reshape(spans * K, width), intra_kv[...]).astype(jnp.bfloat16)
        mine_normed = normed[:, :, pl.ds(own, share), :].reshape(spans * owned, width)
        query = query_rows(mine_normed, intra_query)
        values = [
            attend_few(
                query[index * owned : (index + 1) * owned],
                pair[index * K : (index + 1) * K, :width],
                pair[index * K : (index + 1) * K, width:],
            )
            for index in range(spans)
        ]
        at = pl.multiple_of(source * spans * owned, spans * owned)
        mixed[pl.ds(at, spans * owned), :] = jnp.concatenate(values, axis=0)
        return 0

    lax.fori_loop(0, devices, attend_source, 0)
    enc_ref[...] = frames[pl.ds(pl.multiple_of(me * count, count), count), :]

    for index in range(9, OPERANDS):
        loads[index].wait()
    batch = total // 2

    def finish_intra(half, _):
        at = pl.multiple_of(half * batch * owned, batch * owned)
        result = rest_rows(
            started[pl.ds(at, batch * owned), :], mixed[pl.ds(at, batch * owned), :], *intra_rest
        )
        table = table_across[pl.ds(pl.multiple_of(half * batch, batch), batch), :]
        table = jnp.concatenate(
            [jnp.broadcast_to(table[c : c + 1], (owned, width)) for c in range(batch)], axis=0
        )
        result = round_rows(round_rows(result) + table)
        for side in range(width // LANES):
            across[side, pl.ds(at, batch * owned), :] = result[
                :, side * LANES : (side + 1) * LANES
            ]
        return 0

    lax.fori_loop(0, 2, finish_intra, 0)

    def send_back(chunk, step):
        other = lax.rem(me + step, devices)
        size = spans * part
        return pltpu.make_async_remote_copy(
            src_ref=back.at[chunk, pl.ds(pl.multiple_of(other * size, TILE), size), :],
            dst_ref=got.at[chunk, me],
            send_sem=back_send.at[chunk, step],
            recv_sem=back_recv.at[chunk, step],
            device_id={"span": other},
            device_id_type=MESH,
        )

    def do_chunk(chunk, _):
        firsts = [half * share + chunk * part for half in range(2)]
        block = jnp.concatenate(
            [strided(across, first + p, total, owned) for first in firsts for p in range(part)],
            axis=0,
        )
        result = round_rows(layer_rows(block, group, bias, *inter_weights))
        size = part * total
        for half, first in enumerate(firsts):
            at = pl.multiple_of(first * total, size)
            for side in range(width // LANES):
                inter[side, pl.ds(at, size), :] = result[
                    half * size : (half + 1) * size, side * LANES : (side + 1) * LANES
                ]
        near = chunk * part * total
        far = (share + chunk * part) * total
        pieces = []
        for span in range(total):
            piece = strided(inter, near + span, part, total)
            if span > 0:
                piece = piece + strided(inter, far + span - 1, part, total)
            pieces.append(piece)
        back[chunk] = jnp.concatenate(pieces, axis=0).astype(jnp.bfloat16)
        for step in range(1, devices):
            send_back(chunk, step).start()
        size = spans * part
        got[chunk, me] = back[chunk, pl.ds(pl.multiple_of(me * size, TILE), size), :]
        return 0

    lax.fori_loop(0, chunks, do_chunk, 0)

    def collect(source):
        pieces = [
            got[chunk, source].astype(jnp.float32).reshape(spans, part, width)
            for chunk in range(chunks)
        ]
        at = pl.multiple_of(source * share, TILE)
        summed_ref[:, pl.ds(at, share), :] = jnp.concatenate(pieces, axis=1).astype(jnp.bfloat16)

    collect(me)
    for step in range(1, devices):
        for chunk in range(chunks):
            send_back(chunk, step).wait_recv()
        collect(lax.rem(me + devices - step, devices))

    def drain_back(chunk, _):
        for step in range(1, devices):
            send_back(chunk, step).wait_send()
        return 0

    for step in range(1, devices):
        send_audio(step).wait_send()
    lax.fori_loop(0, chunks, drain_back, 0)


def kernel_body(devices, audio, w_enc, *weights):
    *layers, w_mask = weights
    width = w_enc.shape[1]
    rows = audio.shape[0] // LANES
    count = audio.shape[0] // STRIDE
    spans = count // HOP
    total = spans * devices
    share = HOP // devices
    chunks = 2
    part = share // chunks
    group = LANES
    operands = (
        audio.reshape(rows, LANES),
        w_enc,
        position_values(K, width),
        position_values(total, width),
        *layers,
    )
    vmem = pl.BlockSpec(memory_space=pltpu.VMEM)
    far = pl.BlockSpec(memory_space=pl.ANY)
    dma = pltpu.SemaphoreType.DMA
    enc, summed = pl.pallas_call(
        functools.partial(separator_kernel, devices, group),
        out_shape=[
            jax.ShapeDtypeStruct((count, width), jnp.bfloat16),
            jax.ShapeDtypeStruct((spans, HOP, width), jnp.bfloat16),
        ],
        in_specs=[far] * len(operands),
        out_specs=[vmem] * 2,
        scratch_shapes=[
            pltpu.VMEM((rows * devices + 2 * HOP * STRIDE // LANES, LANES), jnp.float32),
            *[pltpu.VMEM(operand.shape, operand.dtype) for operand in operands[1:]],
            pltpu.VMEM((total * HOP + HOP, width), jnp.bfloat16),
            pltpu.VMEM((spans, K // HOP, HOP, width), jnp.bfloat16),
            pltpu.VMEM((total * 2 * share, width), jnp.float32),
            pltpu.VMEM((total * 2 * share, width), jnp.bfloat16),
            pltpu.VMEM((width // LANES, total * 2 * share, LANES), jnp.float32),
            pltpu.VMEM((width // LANES, total * 2 * share, LANES), jnp.float32),
            pltpu.VMEM((chunks, total * part, width), jnp.bfloat16),
            pltpu.VMEM((chunks, devices, spans * part, width), jnp.bfloat16),
            dma((devices,)),
            dma((devices,)),
            dma((chunks, devices)),
            dma((chunks, devices)),
            dma((len(operands),)),
        ],
        compiler_params=pltpu.CompilerParams(
            collective_id=0, has_side_effects=True, vmem_limit_bytes=60 * 2**20
        ),
    )(*operands)
    summed = summed.reshape(count, width)
    mask = jax.nn.relu(jnp.dot(summed, w_mask, preferred_element_type=jnp.float32))
    repeated = jnp.concatenate([enc] * SPK, axis=1).astype(jnp.float32)
    return (mask * repeated).astype(jnp.bfloat16)


def fits_kernel(devices, count):
    spans = count // HOP
    share = HOP // devices
    return (
        HOP % devices == 0
        and share % TILE == 0
        and LANES % (spans * devices) == 0
        and spans >= 4
        and spans % 2 == 0
        and devices > 1
    )


def body(audio, w_enc, *weights):
    devices = lax.axis_size("span")
    if fits_kernel(devices, audio.shape[0] // STRIDE):
        return kernel_body(devices, audio, w_enc, *weights)
    return plain_body(audio, w_enc, *weights)


def solution(mesh):
    placed = (P(("mix", "span")), P(), P(), P(), P(), P(), P(), P(), P(), P(), P(), P(), P())
    return jax.shard_map(
        body, mesh=mesh, in_specs=placed, out_specs=P(("mix", "span"), None), check_vma=False
    )
```

```python
import functools
import math

import jax
import jax.numpy as jnp
import numpy as np
from jax import lax
from jax.experimental import pallas as pl
from jax.experimental.pallas import tpu as pltpu
from jax.sharding import PartitionSpec as P

HEADS = 8
K = 256
HOP = 128
STRIDE = 8
SPK = 2


def shifted_2(block, axis, distance):
    devices = range(lax.axis_size(axis))
    route = [(i - distance, i) for i in devices if i - distance in devices]
    return lax.ppermute(block, axis, route)


def norm_rows(values):
    center = values - jnp.mean(values, axis=-1, keepdims=True)
    spread = jnp.mean(center * center, axis=-1, keepdims=True)
    return center * lax.rsqrt(spread + 1e-05)


def positions_table(count, width):
    place = jnp.arange(count, dtype=jnp.float32)[:, None]
    index = jnp.arange(width // 2, dtype=jnp.float32)[None, :]
    angle = place * jnp.exp(-math.log(10000.0) * 2.0 * index / width)
    return jnp.concatenate([jnp.sin(angle), jnp.cos(angle)], axis=1)


def matmul(rows, weight):
    shape = rows.shape
    flat = rows.reshape(-1, shape[-1])
    result = jnp.dot(flat, weight, preferred_element_type=jnp.float32)
    return result.reshape(shape[:-1] + (weight.shape[1],))


def attend_block(items):
    query_vectors, key_matrix_rows, value_matrix_rows = items
    score_scale = 1.0 / math.sqrt(query_vectors.shape[-1])
    logit_scores = (
        jnp.einsum(
            "blhd,bmhd->bhlm", query_vectors, key_matrix_rows, preferred_element_type=jnp.float32
        )
        * score_scale
    )
    logit_scores = logit_scores - jnp.max(logit_scores, axis=-1, keepdims=True)
    softmax_weights = jnp.exp(logit_scores)
    softmax_weights = (softmax_weights / jnp.sum(softmax_weights, axis=-1, keepdims=True)).astype(
        jnp.bfloat16
    )
    return jnp.einsum(
        "bhlm,bmhd->blhd", softmax_weights, value_matrix_rows, preferred_element_type=jnp.float32
    ).astype(jnp.bfloat16)


def layer(inputs, w_query, w_kv, w_out, w_up, w_down):
    batch, length, width = inputs.shape
    depth = width // HEADS
    group = math.gcd(batch, max(1, 1024 // length))
    blocks = batch // group
    normed = norm_rows(inputs.astype(jnp.float32)).astype(jnp.bfloat16)
    query_vectors = (
        matmul(normed, w_query).astype(jnp.bfloat16).reshape(blocks, group, length, HEADS, depth)
    )
    pair = matmul(normed, w_kv).astype(jnp.bfloat16)
    key_matrix_rows = pair[..., :width].reshape(blocks, group, length, HEADS, depth)
    value_matrix_rows = pair[..., width:].reshape(blocks, group, length, HEADS, depth)
    mixed = lax.map(attend_block, (query_vectors, key_matrix_rows, value_matrix_rows)).reshape(
        batch, length, width
    )
    middle_value = (inputs.astype(jnp.float32) + matmul(mixed, w_out)).astype(jnp.bfloat16)
    second_operand = norm_rows(middle_value.astype(jnp.float32)).astype(jnp.bfloat16)
    hidden = jax.nn.relu(matmul(second_operand, w_up)).astype(jnp.bfloat16)
    return (middle_value.astype(jnp.float32) + matmul(hidden, w_down)).astype(jnp.bfloat16)


def encode_rows(samples, w_enc):
    blocks = samples.reshape(-1, STRIDE)
    frames = jnp.concatenate([blocks[:-1], blocks[1:]], axis=1)
    result = jnp.dot(
        frames, w_enc, precision=lax.Precision.HIGHEST, preferred_element_type=jnp.float32
    )
    return jax.nn.relu(result).astype(jnp.bfloat16)


def plain_body(
    audio,
    w_enc,
    intra_query,
    intra_kv,
    intra_out,
    intra_up,
    intra_down,
    inter_query,
    inter_kv,
    inter_out,
    inter_up,
    inter_down,
    w_mask,
):
    frame_count = audio.shape[0] // STRIDE
    width = w_enc.shape[1]
    local_spans = frame_count // HOP
    devices = lax.axis_size("span")
    extra = shifted_2(audio[: (HOP + 1) * STRIDE], "span", -1)
    padded = encode_rows(jnp.concatenate([audio, extra], axis=0), w_enc)
    enc = padded[:frame_count]
    spans = jnp.concatenate(
        [
            padded[:frame_count].reshape(local_spans, HOP, width),
            padded[HOP:].reshape(local_spans, HOP, width),
        ],
        axis=1,
    )
    start = (spans.astype(jnp.float32) + positions_table(K, width)[None]).astype(jnp.bfloat16)
    intra = layer(start, intra_query, intra_kv, intra_out, intra_up, intra_down)
    per_device = K // devices
    grouped = intra.reshape(local_spans, devices, per_device, width)
    gathered = lax.all_to_all(grouped, "span", split_axis=1, concat_axis=0, tiled=True)
    total = gathered.shape[0]
    plain = gathered[:, 0]
    shifted = (plain.astype(jnp.float32) + positions_table(total, width)[:, None, :]).astype(
        jnp.bfloat16
    )
    turned = jnp.transpose(shifted, (1, 0, 2))
    result = layer(turned, inter_query, inter_kv, inter_out, inter_up, inter_down)
    inter = jnp.transpose(result, (1, 0, 2))[:, None]
    back = lax.all_to_all(inter, "span", split_axis=0, concat_axis=1, tiled=True).reshape(
        local_spans, K, width
    )
    second_half = back[:, HOP:]
    carried = shifted_2(second_half[-1], "span", 1)
    earlier = jnp.concatenate([carried[None], second_half[:-1]], axis=0)
    summed = back[:, :HOP].astype(jnp.float32) + earlier.astype(jnp.float32)
    summed = summed.reshape(frame_count, width).astype(jnp.bfloat16)
    mask = jax.nn.relu(jnp.dot(summed, w_mask, preferred_element_type=jnp.float32))
    repeated = jnp.concatenate([enc] * SPK, axis=1).astype(jnp.float32)
    return (mask * repeated).astype(jnp.bfloat16)


LANES = 128
TILE = 16
OPERANDS = 15
MESH = pl.DeviceIdType.MESH


def position_values(count, width):
    place = np.arange(count, dtype=np.float64)[:, None]
    index = np.arange(width // 2, dtype=np.float64)[None, :]
    angle = place * np.exp(-math.log(10000.0) * 2.0 * index / width)
    return np.concatenate([np.sin(angle), np.cos(angle)], axis=1).astype(np.float32)


def dot(left, right):
    return jnp.dot(left, right, preferred_element_type=jnp.float32)


def round_rows(values):
    return values.astype(jnp.bfloat16).astype(jnp.float32)


def strided(ref, first, count, stride):
    picked = [ref[side, pl.ds(first, count, stride=stride), :] for side in range(ref.shape[0])]
    return jnp.concatenate(picked, axis=1)


def attend_rows(query, key, value, bias):
    rows, width = query.shape
    depth = width // HEADS
    owner = lax.broadcasted_iota(jnp.int32, (1, LANES), 1) // depth
    zero = jnp.zeros((), jnp.bfloat16)
    ones = jnp.ones((key.shape[0], LANES), jnp.bfloat16)
    heads = LANES // depth
    sides = []
    for at in range(0, width, LANES):
        side_query, side_key, side_value = (
            block[:, at : at + LANES] for block in (query, key, value)
        )
        scores = lax.dot_general(
            jnp.concatenate(
                [jnp.where(owner == head, side_query, zero) for head in range(heads)], axis=0
            ),
            side_key,
            (((1,), (1,)), ((), ())),
            preferred_element_type=jnp.float32,
        )
        if bias is not None:
            scores = scores + jnp.concatenate([bias] * heads, axis=0)
        scores = scores - jnp.max(scores, axis=-1, keepdims=True)
        weights = jnp.exp2(scores.astype(jnp.bfloat16))
        result = dot(weights, jnp.concatenate([side_value, ones], axis=1))
        owners = jnp.concatenate([owner, owner], axis=1)
        total = result[:rows]
        for head in range(1, heads):
            total = jnp.where(owners == head, result[head * rows : (head + 1) * rows], total)
        sides.append(total[:, :LANES] / total[:, LANES:])
    return jnp.concatenate(sides, axis=1).astype(jnp.bfloat16)


def query_rows(normed, w_query):
    scale = math.log2(math.e) / math.sqrt(normed.shape[1] // HEADS)
    return (dot(normed, w_query[...]) * scale).astype(jnp.bfloat16)


def rest_rows(rows, mixed, w_out, w_up, w_down):
    middle = round_rows(rows + dot(mixed, w_out[...]))
    second = norm_rows(middle).astype(jnp.bfloat16)
    hidden = jnp.maximum(dot(second, w_up[...]), 0.0).astype(jnp.bfloat16)
    return middle + dot(hidden, w_down[...])


def layer_rows(rows, group, bias, w_query, w_kv, w_out, w_up, w_down):
    width = rows.shape[1]
    normed = norm_rows(rows).astype(jnp.bfloat16)
    query = query_rows(normed, w_query)
    pair = dot(normed, w_kv[...]).astype(jnp.bfloat16)
    mixed = [
        attend_rows(
            query[at : at + group],
            pair[at : at + group, :width],
            pair[at : at + group, width:],
            bias,
        )
        for at in range(0, rows.shape[0], group)
    ]
    return rest_rows(rows, jnp.concatenate(mixed, axis=0), w_out, w_up, w_down)


def separator_kernel(devices, group, *refs):
    given, refs = refs[:OPERANDS], refs[OPERANDS:]
    out_ref, refs = refs[0], refs[1:]
    held, refs = refs[:OPERANDS], refs[OPERANDS:]
    audio = given[0]
    samples, w_enc, table_span, table_across, *layers = held
    intra_query, intra_kv, *intra_rest = layers[:5]
    inter_weights = layers[5:10]
    w_mask = layers[10]
    (
        frames,
        normed,
        sent,
        taken,
        across,
        inter,
        back,
        got,
        audio_send,
        audio_recv,
        halo_send,
        halo_recv,
        out_send,
        out_recv,
        back_send,
        back_recv,
        load,
    ) = refs
    me = lax.axis_index("span")
    width = w_enc.shape[1]
    rows = audio.shape[0]
    per_row = LANES // STRIDE
    count = rows * per_row
    spans = count // HOP
    share = HOP // devices
    owned = 2 * share
    total = spans * devices
    chunks = back.shape[0]
    part = share // chunks
    members = devices // 2
    half_hop = HOP // 2
    halo_rows = samples.shape[1] - rows
    partner = lax.rem(me + members, devices)
    group_at = me // members
    member = lax.rem(me, members)

    loads = []
    for index in range(OPERANDS):
        target = samples.at[0, pl.ds(0, rows)] if index == 0 else held[index]
        loads.append(pltpu.make_async_copy(given[index], target, load.at[index]))
        loads[-1].start()

    barrier = pltpu.get_barrier_semaphore()
    for step in range(1, devices):
        other = lax.rem(me + step, devices)
        pl.semaphore_signal(barrier, inc=1, device_id={"span": other}, device_id_type=MESH)

    def send_halo(section):
        other = lax.rem(me + devices - 1 + section * members, devices)
        return pltpu.make_async_remote_copy(
            src_ref=audio.at[pl.ds(0, halo_rows)],
            dst_ref=samples.at[section, pl.ds(rows, halo_rows)],
            send_sem=halo_send.at[section],
            recv_sem=halo_recv.at[section],
            device_id={"span": other},
            device_id_type=MESH,
        )

    send_audio = pltpu.make_async_remote_copy(
        src_ref=audio,
        dst_ref=samples.at[1, pl.ds(0, rows)],
        send_sem=audio_send,
        recv_sem=audio_recv,
        device_id={"span": partner},
        device_id_type=MESH,
    )

    lane = lax.broadcasted_iota(jnp.int32, (1, LANES), 1)
    slot = lax.broadcasted_iota(jnp.int32, (HOP, 1), 0) % per_row
    mine = lane // STRIDE == slot
    for index in range(4):
        loads[index].wait()
    w_low = jnp.concatenate([w_enc[:STRIDE]] * per_row, axis=0)
    w_high = jnp.concatenate([w_enc[STRIDE:]] * per_row, axis=0)
    w_both = jnp.concatenate([w_low, w_high], axis=0)
    w_lead = w_both.astype(jnp.bfloat16)
    w_rest = (w_both - w_lead.astype(jnp.float32)).astype(jnp.bfloat16)
    step_rows = HOP // per_row
    kind = [lax.broadcasted_iota(jnp.int32, (group, group), axis) // total for axis in (0, 1)]
    bias = jnp.where(kind[0] == kind[1], 0.0, -1e30)

    def encode(section, hop):
        at = hop * step_rows
        low = samples[section, pl.ds(at, step_rows), :]
        turned = pltpu.roll(samples[section, pl.ds(at, 2 * step_rows), :], LANES - STRIDE, 1)
        high = jnp.where(lane < LANES - STRIDE, turned[:step_rows], turned[1 : step_rows + 1])
        leads = []
        rests = []
        for block in (low, high):
            lead = block.astype(jnp.bfloat16).astype(jnp.float32)
            for values, into in ((lead, leads), (block - lead, rests)):
                spread = jnp.concatenate(
                    [
                        jnp.broadcast_to(values[r : r + 1], (per_row, LANES))
                        for r in range(step_rows)
                    ],
                    axis=0,
                )
                into.append(jnp.where(mine, spread, 0.0).astype(jnp.bfloat16))
        lead = jnp.concatenate(leads, axis=1)
        rest = jnp.concatenate(rests, axis=1)
        result = dot(lead, w_lead) + (dot(rest, w_lead) + dot(lead, w_rest))
        frames[section, pl.ds(hop * HOP, HOP), :] = jnp.maximum(result, 0.0).astype(jnp.bfloat16)

    for hop in range(spans - 1):
        encode(0, hop)
    pl.semaphore_wait(barrier, devices - 1)
    send_halo(0).start()
    send_audio.start()
    send_halo(1).start()
    for index in range(4, 9):
        loads[index].wait()
    near = pl.multiple_of(group_at * half_hop, half_hop)

    def send_out(section, step):
        other = lax.rem(member + step, members)
        source = lax.rem(me + section * members, devices)
        return pltpu.make_async_remote_copy(
            src_ref=sent.at[section, :, :, pl.ds(pl.multiple_of(other * share, TILE), share), :],
            dst_ref=taken.at[pl.ds(source * spans, spans)],
            send_sem=out_send.at[section, step],
            recv_sem=out_recv.at[section, step],
            device_id={"span": group_at * members + other},
            device_id_type=MESH,
        )

    def do_section(section, _):
        source = lax.rem(me + section * members, devices)

        @pl.when(section == 1)
        def _():
            send_audio.wait_recv()
            for hop in range(spans - 1):
                encode(1, hop)

        send_halo(section).wait_recv()

        @pl.when(source == devices - 1)
        def _():
            samples[section, rows:] = jnp.zeros((halo_rows, LANES), jnp.float32)

        encode(section, spans - 1)
        encode(section, spans)
        starts = []
        for index in range(spans):
            start = frames[section, pl.ds(index * HOP, K), :].astype(jnp.float32)
            start = round_rows(start + table_span[...])
            values = norm_rows(start).astype(jnp.bfloat16)
            normed[index] = values.reshape(K // HOP, HOP, width)
            for half in range(K // HOP):
                at = pl.multiple_of(index * HOP + half * HOP + near, half_hop)
                start = frames[section, pl.ds(at, half_hop), :].astype(jnp.float32)
                at = pl.multiple_of(half * HOP + near, half_hop)
                starts.append(round_rows(start + table_span[pl.ds(at, half_hop), :]))
        pair = dot(normed[...].reshape(spans * K, width), intra_kv[...]).astype(jnp.bfloat16)
        mine_normed = normed[:, :, pl.ds(near, half_hop), :].reshape(spans * HOP, width)
        query = query_rows(mine_normed, intra_query)
        mixed = [
            attend_rows(
                query[index * HOP : (index + 1) * HOP],
                pair[index * K : (index + 1) * K, :width],
                pair[index * K : (index + 1) * K, width:],
                None,
            )
            for index in range(spans)
        ]
        result = rest_rows(
            jnp.concatenate(starts, axis=0), jnp.concatenate(mixed, axis=0), *intra_rest
        )
        result = result.astype(jnp.bfloat16)
        sent[section] = result.reshape(spans, K // HOP, half_hop, width)
        for step in range(1, members):
            send_out(section, step).start()
        at = pl.multiple_of(member * share, TILE)
        taken[pl.ds(source * spans, spans)] = sent[section, :, :, pl.ds(at, share), :]
        return 0

    lax.fori_loop(0, 2, do_section, 0)

    for index in range(9, OPERANDS):
        loads[index].wait()

    def place(source):
        for index in range(spans):
            row = source * spans + index
            block = taken[row].reshape(owned, width).astype(jnp.float32)
            at = pl.multiple_of(row * owned, owned)
            block = round_rows(block + table_across[pl.ds(row, 1), :])
            for side in range(width // LANES):
                across[side, pl.ds(at, owned), :] = block[:, side * LANES : (side + 1) * LANES]

    def place_section(section, _):
        place(lax.rem(me + section * members, devices))
        for step in range(1, members):
            send_out(section, step).wait_recv()
            other = group_at * members + lax.rem(member + members - step, members)
            place(lax.rem(other + section * members, devices))
        return 0

    lax.fori_loop(0, 2, place_section, 0)

    def send_back(chunk, step):
        other = lax.rem(me + step, devices)
        size = spans * part
        return pltpu.make_async_remote_copy(
            src_ref=back.at[chunk, pl.ds(pl.multiple_of(other * size, TILE), size), :],
            dst_ref=got.at[chunk, me],
            send_sem=back_send.at[chunk, step],
            recv_sem=back_recv.at[chunk, step],
            device_id={"span": other},
            device_id_type=MESH,
        )

    def do_chunk(chunk, _):
        firsts = [half * share + chunk * part for half in range(2)]
        block = jnp.concatenate(
            [strided(across, first + p, total, owned) for first in firsts for p in range(part)],
            axis=0,
        )
        result = round_rows(layer_rows(block, group, bias, *inter_weights))
        size = part * total
        for half, first in enumerate(firsts):
            at = pl.multiple_of(first * total, size)
            for side in range(width // LANES):
                inter[side, pl.ds(at, size), :] = result[
                    half * size : (half + 1) * size, side * LANES : (side + 1) * LANES
                ]
        near = chunk * part * total
        far = (share + chunk * part) * total
        pieces = []
        for span in range(total):
            piece = strided(inter, near + span, part, total)
            if span > 0:
                piece = piece + strided(inter, far + span - 1, part, total)
            pieces.append(piece)
        back[chunk] = jnp.concatenate(pieces, axis=0).astype(jnp.bfloat16)
        for step in range(1, devices):
            send_back(chunk, step).start()
        size = spans * part
        got[chunk, me] = back[chunk, pl.ds(pl.multiple_of(me * size, TILE), size), :]
        return 0

    lax.fori_loop(0, chunks, do_chunk, 0)

    def collect(source):
        pieces = [
            got[chunk, source].astype(jnp.float32).reshape(spans, part, width)
            for chunk in range(chunks)
        ]
        summed = jnp.concatenate(pieces, axis=1).reshape(spans * share, width)
        mask = jnp.maximum(dot(summed.astype(jnp.bfloat16), w_mask[...]), 0.0)
        at = pl.multiple_of(source * share, TILE)
        enc = [frames[0, pl.ds(span * HOP + at, share), :] for span in range(spans)]
        enc = jnp.concatenate(enc, axis=0).astype(jnp.float32)
        out = mask * jnp.concatenate([enc] * SPK, axis=1)
        out = out.astype(jnp.bfloat16).reshape(spans, share, SPK * width)
        out_ref[:, pl.ds(at, share), :] = out

    collect(me)
    for step in range(1, devices):
        for chunk in range(chunks):
            send_back(chunk, step).wait_recv()
        collect(lax.rem(me + devices - step, devices))

    def drain_back(chunk, _):
        for step in range(1, devices):
            send_back(chunk, step).wait_send()
        return 0

    send_audio.wait_send()
    for section in range(2):
        send_halo(section).wait_send()
        for step in range(1, members):
            send_out(section, step).wait_send()
    lax.fori_loop(0, chunks, drain_back, 0)


def kernel_body(devices, audio, w_enc, *weights):
    width = w_enc.shape[1]
    rows = audio.shape[0] // LANES
    count = audio.shape[0] // STRIDE
    spans = count // HOP
    total = spans * devices
    share = HOP // devices
    chunks = 2
    part = share // chunks
    group = LANES
    operands = (
        audio.reshape(rows, LANES),
        w_enc,
        position_values(K, width),
        position_values(total, width),
        *weights,
    )
    vmem = pl.BlockSpec(memory_space=pltpu.VMEM)
    far = pl.BlockSpec(memory_space=pl.ANY)
    dma = pltpu.SemaphoreType.DMA
    separated = pl.pallas_call(
        functools.partial(separator_kernel, devices, group),
        out_shape=jax.ShapeDtypeStruct((spans, HOP, SPK * width), jnp.bfloat16),
        in_specs=[far] * len(operands),
        out_specs=vmem,
        scratch_shapes=[
            pltpu.VMEM((2, rows + 2 * HOP * STRIDE // LANES, LANES), jnp.float32),
            *[pltpu.VMEM(operand.shape, operand.dtype) for operand in operands[1:]],
            pltpu.VMEM((2, count + HOP, width), jnp.bfloat16),
            pltpu.VMEM((spans, K // HOP, HOP, width), jnp.bfloat16),
            pltpu.VMEM((2, spans, K // HOP, HOP // 2, width), jnp.bfloat16),
            pltpu.VMEM((total, K // HOP, share, width), jnp.bfloat16),
            pltpu.VMEM((width // LANES, total * 2 * share, LANES), jnp.float32),
            pltpu.VMEM((width // LANES, total * 2 * share, LANES), jnp.float32),
            pltpu.VMEM((chunks, total * part, width), jnp.bfloat16),
            pltpu.VMEM((chunks, devices, spans * part, width), jnp.bfloat16),
            dma,
            dma,
            dma((2,)),
            dma((2,)),
            dma((2, devices // 2)),
            dma((2, devices // 2)),
            dma((chunks, devices)),
            dma((chunks, devices)),
            dma((len(operands),)),
        ],
        compiler_params=pltpu.CompilerParams(
            collective_id=0, has_side_effects=True, vmem_limit_bytes=60 * 2**20
        ),
    )(*operands)
    return separated.reshape(count, SPK * width)


def fits_kernel(devices, count):
    spans = count // HOP
    share = HOP // devices
    return (
        HOP % devices == 0
        and share % TILE == 0
        and LANES % (spans * devices) == 0
        and share * (devices // 2) == HOP // 2
        and spans >= 4
        and spans % 2 == 0
        and devices % 2 == 0
    )


def body(audio, w_enc, *weights):
    devices = lax.axis_size("span")
    if fits_kernel(devices, audio.shape[0] // STRIDE):
        return kernel_body(devices, audio, w_enc, *weights)
    return plain_body(audio, w_enc, *weights)


def solution(mesh):
    placed = (P(("mix", "span")), P(), P(), P(), P(), P(), P(), P(), P(), P(), P(), P(), P())
    return jax.shard_map(
        body, mesh=mesh, in_specs=placed, out_specs=P(("mix", "span"), None), check_vma=False
    )
```

```python
import functools
import math

import jax
import jax.numpy as jnp
import numpy as np
from jax import lax
from jax.experimental import pallas as pl
from jax.experimental.pallas import tpu as pltpu
from jax.sharding import PartitionSpec as P

HEADS = 8
K = 256
HOP = 128
STRIDE = 8
SPK = 2


def shifted_2(block, axis, distance):
    devices = range(lax.axis_size(axis))
    route = [(i - distance, i) for i in devices if i - distance in devices]
    return lax.ppermute(block, axis, route)


def norm_rows(values):
    center = values - jnp.mean(values, axis=-1, keepdims=True)
    spread = jnp.mean(center * center, axis=-1, keepdims=True)
    return center * lax.rsqrt(spread + 1e-05)


def positions_table(count, width):
    place = jnp.arange(count, dtype=jnp.float32)[:, None]
    index = jnp.arange(width // 2, dtype=jnp.float32)[None, :]
    angle = place * jnp.exp(-math.log(10000.0) * 2.0 * index / width)
    return jnp.concatenate([jnp.sin(angle), jnp.cos(angle)], axis=1)


def matmul(rows, weight):
    shape = rows.shape
    flat = rows.reshape(-1, shape[-1])
    result = jnp.dot(flat, weight, preferred_element_type=jnp.float32)
    return result.reshape(shape[:-1] + (weight.shape[1],))


def attend_block(items):
    query_vectors, key_matrix_rows, value_matrix_rows = items
    score_scale = 1.0 / math.sqrt(query_vectors.shape[-1])
    logit_scores = (
        jnp.einsum(
            "blhd,bmhd->bhlm", query_vectors, key_matrix_rows, preferred_element_type=jnp.float32
        )
        * score_scale
    )
    logit_scores = logit_scores - jnp.max(logit_scores, axis=-1, keepdims=True)
    softmax_weights = jnp.exp(logit_scores)
    softmax_weights = (softmax_weights / jnp.sum(softmax_weights, axis=-1, keepdims=True)).astype(
        jnp.bfloat16
    )
    return jnp.einsum(
        "bhlm,bmhd->blhd", softmax_weights, value_matrix_rows, preferred_element_type=jnp.float32
    ).astype(jnp.bfloat16)


def layer(inputs, w_query, w_kv, w_out, w_up, w_down):
    batch, length, width = inputs.shape
    depth = width // HEADS
    group = math.gcd(batch, max(1, 1024 // length))
    blocks = batch // group
    normed = norm_rows(inputs.astype(jnp.float32)).astype(jnp.bfloat16)
    query_vectors = (
        matmul(normed, w_query).astype(jnp.bfloat16).reshape(blocks, group, length, HEADS, depth)
    )
    pair = matmul(normed, w_kv).astype(jnp.bfloat16)
    key_matrix_rows = pair[..., :width].reshape(blocks, group, length, HEADS, depth)
    value_matrix_rows = pair[..., width:].reshape(blocks, group, length, HEADS, depth)
    mixed = lax.map(attend_block, (query_vectors, key_matrix_rows, value_matrix_rows)).reshape(
        batch, length, width
    )
    middle_value = (inputs.astype(jnp.float32) + matmul(mixed, w_out)).astype(jnp.bfloat16)
    second_operand = norm_rows(middle_value.astype(jnp.float32)).astype(jnp.bfloat16)
    hidden = jax.nn.relu(matmul(second_operand, w_up)).astype(jnp.bfloat16)
    return (middle_value.astype(jnp.float32) + matmul(hidden, w_down)).astype(jnp.bfloat16)


def encode_rows(samples, w_enc):
    blocks = samples.reshape(-1, STRIDE)
    frames = jnp.concatenate([blocks[:-1], blocks[1:]], axis=1)
    result = jnp.dot(
        frames, w_enc, precision=lax.Precision.HIGHEST, preferred_element_type=jnp.float32
    )
    return jax.nn.relu(result).astype(jnp.bfloat16)


def plain_body(
    audio,
    w_enc,
    intra_query,
    intra_kv,
    intra_out,
    intra_up,
    intra_down,
    inter_query,
    inter_kv,
    inter_out,
    inter_up,
    inter_down,
    w_mask,
):
    frame_count = audio.shape[0] // STRIDE
    width = w_enc.shape[1]
    local_spans = frame_count // HOP
    devices = lax.axis_size("span")
    extra = shifted_2(audio[: (HOP + 1) * STRIDE], "span", -1)
    padded = encode_rows(jnp.concatenate([audio, extra], axis=0), w_enc)
    enc = padded[:frame_count]
    spans = jnp.concatenate(
        [
            padded[:frame_count].reshape(local_spans, HOP, width),
            padded[HOP:].reshape(local_spans, HOP, width),
        ],
        axis=1,
    )
    start = (spans.astype(jnp.float32) + positions_table(K, width)[None]).astype(jnp.bfloat16)
    intra = layer(start, intra_query, intra_kv, intra_out, intra_up, intra_down)
    per_device = K // devices
    grouped = intra.reshape(local_spans, devices, per_device, width)
    gathered = lax.all_to_all(grouped, "span", split_axis=1, concat_axis=0, tiled=True)
    total = gathered.shape[0]
    plain = gathered[:, 0]
    shifted = (plain.astype(jnp.float32) + positions_table(total, width)[:, None, :]).astype(
        jnp.bfloat16
    )
    turned = jnp.transpose(shifted, (1, 0, 2))
    result = layer(turned, inter_query, inter_kv, inter_out, inter_up, inter_down)
    inter = jnp.transpose(result, (1, 0, 2))[:, None]
    back = lax.all_to_all(inter, "span", split_axis=0, concat_axis=1, tiled=True).reshape(
        local_spans, K, width
    )
    second_half = back[:, HOP:]
    carried = shifted_2(second_half[-1], "span", 1)
    earlier = jnp.concatenate([carried[None], second_half[:-1]], axis=0)
    summed = back[:, :HOP].astype(jnp.float32) + earlier.astype(jnp.float32)
    summed = summed.reshape(frame_count, width).astype(jnp.bfloat16)
    mask = jax.nn.relu(jnp.dot(summed, w_mask, preferred_element_type=jnp.float32))
    repeated = jnp.concatenate([enc] * SPK, axis=1).astype(jnp.float32)
    return (mask * repeated).astype(jnp.bfloat16)


LANES = 128
TILE = 16
OPERANDS = 15
MESH = pl.DeviceIdType.MESH


def position_values(count, width):
    place = np.arange(count, dtype=np.float64)[:, None]
    index = np.arange(width // 2, dtype=np.float64)[None, :]
    angle = place * np.exp(-math.log(10000.0) * 2.0 * index / width)
    return np.concatenate([np.sin(angle), np.cos(angle)], axis=1).astype(np.float32)


def dot(left, right):
    return jnp.dot(left, right, preferred_element_type=jnp.float32)


def norm_wide(rows):
    width = rows.shape[1]
    ones = jnp.ones((width, LANES), jnp.bfloat16)
    mean = dot(rows.astype(jnp.bfloat16), ones) * (1.0 / width)
    center = [rows[:, at : at + LANES] - mean for at in range(0, width, LANES)]
    squares = jnp.concatenate([(part * part).astype(jnp.bfloat16) for part in center], axis=1)
    scale = lax.rsqrt(dot(squares, ones) * (1.0 / width) + 1e-05)
    return jnp.concatenate([part * scale for part in center], axis=1)


def round_rows(values):
    return values.astype(jnp.bfloat16).astype(jnp.float32)


def strided(ref, first, count, stride):
    picked = [ref[side, pl.ds(first, count, stride=stride), :] for side in range(ref.shape[0])]
    return jnp.concatenate(picked, axis=1)


def attend_rows(query, key, value, bias):
    rows, width = query.shape
    depth = width // HEADS
    owner = lax.broadcasted_iota(jnp.int32, (1, LANES), 1) // depth
    zero = jnp.zeros((), jnp.bfloat16)
    ones = jnp.ones((key.shape[0], LANES), jnp.bfloat16)
    heads = LANES // depth
    sides = []
    for at in range(0, width, LANES):
        side_query, side_key, side_value = (
            block[:, at : at + LANES] for block in (query, key, value)
        )
        scores = lax.dot_general(
            jnp.concatenate(
                [jnp.where(owner == head, side_query, zero) for head in range(heads)], axis=0
            ),
            side_key,
            (((1,), (1,)), ((), ())),
            preferred_element_type=jnp.float32,
        )
        if bias is not None:
            scores = scores + jnp.concatenate([bias] * heads, axis=0)
        scores = scores - jnp.max(scores, axis=-1, keepdims=True)
        weights = jnp.exp2(scores.astype(jnp.bfloat16))
        result = dot(weights, jnp.concatenate([side_value, ones], axis=1))
        owners = jnp.concatenate([owner, owner], axis=1)
        total = result[:rows]
        for head in range(1, heads):
            total = jnp.where(owners == head, result[head * rows : (head + 1) * rows], total)
        sides.append(total[:, :LANES] / total[:, LANES:])
    return jnp.concatenate(sides, axis=1).astype(jnp.bfloat16)


def query_rows(normed, w_query):
    scale = math.log2(math.e) / math.sqrt(normed.shape[1] // HEADS)
    return (dot(normed, w_query[...]) * scale).astype(jnp.bfloat16)


def rest_rows(rows, mixed, w_out, w_up, w_down):
    middle = round_rows(rows + dot(mixed, w_out[...]))
    second = norm_wide(middle).astype(jnp.bfloat16)
    hidden = jnp.maximum(dot(second, w_up[...]), 0.0).astype(jnp.bfloat16)
    return middle + dot(hidden, w_down[...])


def layer_rows(rows, group, bias, w_query, w_kv, w_out, w_up, w_down):
    width = rows.shape[1]
    normed = norm_wide(rows).astype(jnp.bfloat16)
    query = query_rows(normed, w_query)
    pair = dot(normed, w_kv[...]).astype(jnp.bfloat16)
    mixed = [
        attend_rows(
            query[at : at + group],
            pair[at : at + group, :width],
            pair[at : at + group, width:],
            bias,
        )
        for at in range(0, rows.shape[0], group)
    ]
    return rest_rows(rows, jnp.concatenate(mixed, axis=0), w_out, w_up, w_down)


def separator_kernel(devices, group, *refs):
    given, refs = refs[:OPERANDS], refs[OPERANDS:]
    out_ref, refs = refs[0], refs[1:]
    held, refs = refs[:OPERANDS], refs[OPERANDS:]
    audio = given[0]
    samples, w_enc, table_span, table_across, *layers = held
    intra_query, intra_kv, *intra_rest = layers[:5]
    inter_weights = layers[5:10]
    w_mask = layers[10]
    (
        frames,
        normed,
        sent,
        taken,
        across,
        inter,
        back,
        got,
        audio_send,
        audio_recv,
        halo_send,
        halo_recv,
        out_send,
        out_recv,
        back_send,
        back_recv,
        load,
    ) = refs
    me = lax.axis_index("span")
    width = w_enc.shape[1]
    rows = audio.shape[0]
    per_row = LANES // STRIDE
    count = rows * per_row
    spans = count // HOP
    share = HOP // devices
    owned = 2 * share
    total = spans * devices
    chunks = back.shape[0]
    part = share // chunks
    members = devices // 2
    half_hop = HOP // 2
    halo_rows = samples.shape[1] - rows
    partner = lax.rem(me + members, devices)
    group_at = me // members
    member = lax.rem(me, members)

    loads = []
    for index in range(OPERANDS):
        target = samples.at[0, pl.ds(0, rows)] if index == 0 else held[index]
        loads.append(pltpu.make_async_copy(given[index], target, load.at[index]))
    for index in range(9):
        loads[index].start()

    barrier = pltpu.get_barrier_semaphore()
    for step in range(1, devices):
        other = lax.rem(me + step, devices)
        pl.semaphore_signal(barrier, inc=1, device_id={"span": other}, device_id_type=MESH)

    def send_halo(section):
        other = lax.rem(me + devices - 1 + section * members, devices)
        return pltpu.make_async_remote_copy(
            src_ref=audio.at[pl.ds(0, halo_rows)],
            dst_ref=samples.at[section, pl.ds(rows, halo_rows)],
            send_sem=halo_send.at[section],
            recv_sem=halo_recv.at[section],
            device_id={"span": other},
            device_id_type=MESH,
        )

    send_audio = pltpu.make_async_remote_copy(
        src_ref=audio,
        dst_ref=samples.at[1, pl.ds(0, rows)],
        send_sem=audio_send,
        recv_sem=audio_recv,
        device_id={"span": partner},
        device_id_type=MESH,
    )

    lane = lax.broadcasted_iota(jnp.int32, (1, LANES), 1)
    slot = lax.broadcasted_iota(jnp.int32, (HOP, 1), 0) % per_row
    mine = lane // STRIDE == slot
    for index in range(4):
        loads[index].wait()
    w_low = jnp.concatenate([w_enc[:STRIDE]] * per_row, axis=0)
    w_high = jnp.concatenate([w_enc[STRIDE:]] * per_row, axis=0)
    w_both = jnp.concatenate([w_low, w_high], axis=0)
    w_lead = w_both.astype(jnp.bfloat16)
    w_rest = (w_both - w_lead.astype(jnp.float32)).astype(jnp.bfloat16)
    step_rows = HOP // per_row
    kind = [lax.broadcasted_iota(jnp.int32, (group, group), axis) // total for axis in (0, 1)]
    bias = jnp.where(kind[0] == kind[1], 0.0, -1e30)

    def encode(section, hop):
        at = hop * step_rows
        low = samples[section, pl.ds(at, step_rows), :]
        turned = pltpu.roll(samples[section, pl.ds(at, 2 * step_rows), :], LANES - STRIDE, 1)
        high = jnp.where(lane < LANES - STRIDE, turned[:step_rows], turned[1 : step_rows + 1])
        leads = []
        rests = []
        for block in (low, high):
            lead = block.astype(jnp.bfloat16).astype(jnp.float32)
            for values, into in ((lead, leads), (block - lead, rests)):
                spread = jnp.concatenate(
                    [
                        jnp.broadcast_to(values[r : r + 1], (per_row, LANES))
                        for r in range(step_rows)
                    ],
                    axis=0,
                )
                into.append(jnp.where(mine, spread, 0.0).astype(jnp.bfloat16))
        lead = jnp.concatenate(leads, axis=1)
        rest = jnp.concatenate(rests, axis=1)
        result = dot(lead, w_lead) + (dot(rest, w_lead) + dot(lead, w_rest))
        frames[section, pl.ds(hop * HOP, HOP), :] = jnp.maximum(result, 0.0).astype(jnp.bfloat16)

    for hop in range(spans - 1):
        encode(0, hop)
    pl.semaphore_wait(barrier, devices - 1)
    send_halo(0).start()
    send_audio.start()
    send_halo(1).start()
    for index in range(4, 9):
        loads[index].wait()
    for index in range(9, OPERANDS):
        loads[index].start()
    near = pl.multiple_of(group_at * half_hop, half_hop)

    def send_out(section, step):
        other = lax.rem(member + step, members)
        source = lax.rem(me + section * members, devices)
        return pltpu.make_async_remote_copy(
            src_ref=sent.at[section, :, :, pl.ds(pl.multiple_of(other * share, TILE), share), :],
            dst_ref=taken.at[pl.ds(source * spans, spans)],
            send_sem=out_send.at[section, step],
            recv_sem=out_recv.at[section, step],
            device_id={"span": group_at * members + other},
            device_id_type=MESH,
        )

    def do_section(section, _):
        source = lax.rem(me + section * members, devices)

        @pl.when(section == 1)
        def _():
            send_audio.wait_recv()
            for hop in range(spans - 1):
                encode(1, hop)

        send_halo(section).wait_recv()

        @pl.when(source == devices - 1)
        def _():
            samples[section, rows:] = jnp.zeros((halo_rows, LANES), jnp.float32)

        encode(section, spans - 1)
        encode(section, spans)
        starts = []
        for index in range(spans):
            start = frames[section, pl.ds(index * HOP, K), :].astype(jnp.float32)
            start = round_rows(start + table_span[...])
            values = norm_wide(start).astype(jnp.bfloat16)
            normed[index] = values.reshape(K // HOP, HOP, width)
            for half in range(K // HOP):
                at = pl.multiple_of(index * HOP + half * HOP + near, half_hop)
                start = frames[section, pl.ds(at, half_hop), :].astype(jnp.float32)
                at = pl.multiple_of(half * HOP + near, half_hop)
                starts.append(round_rows(start + table_span[pl.ds(at, half_hop), :]))
        pair = dot(normed[...].reshape(spans * K, width), intra_kv[...]).astype(jnp.bfloat16)
        mine_normed = normed[:, :, pl.ds(near, half_hop), :].reshape(spans * HOP, width)
        query = query_rows(mine_normed, intra_query)
        mixed = [
            attend_rows(
                query[index * HOP : (index + 1) * HOP],
                pair[index * K : (index + 1) * K, :width],
                pair[index * K : (index + 1) * K, width:],
                None,
            )
            for index in range(spans)
        ]
        result = rest_rows(
            jnp.concatenate(starts, axis=0), jnp.concatenate(mixed, axis=0), *intra_rest
        )
        result = result.astype(jnp.bfloat16)
        sent[section] = result.reshape(spans, K // HOP, half_hop, width)
        for step in range(1, members):
            send_out(section, step).start()
        at = pl.multiple_of(member * share, TILE)
        taken[pl.ds(source * spans, spans)] = sent[section, :, :, pl.ds(at, share), :]
        return 0

    lax.fori_loop(0, 2, do_section, 0)

    for index in range(9, OPERANDS):
        loads[index].wait()

    def place(source):
        for index in range(spans):
            row = source * spans + index
            block = taken[row].reshape(owned, width).astype(jnp.float32)
            at = pl.multiple_of(row * owned, owned)
            block = round_rows(block + table_across[pl.ds(row, 1), :])
            for side in range(width // LANES):
                across[side, pl.ds(at, owned), :] = block[:, side * LANES : (side + 1) * LANES]

    def place_section(section, _):
        place(lax.rem(me + section * members, devices))
        for step in range(1, members):
            send_out(section, step).wait_recv()
            other = group_at * members + lax.rem(member + members - step, members)
            place(lax.rem(other + section * members, devices))
        return 0

    lax.fori_loop(0, 2, place_section, 0)

    def send_back(chunk, step):
        other = lax.rem(me + step, devices)
        size = spans * part
        return pltpu.make_async_remote_copy(
            src_ref=back.at[chunk, pl.ds(pl.multiple_of(other * size, TILE), size), :],
            dst_ref=got.at[chunk, me],
            send_sem=back_send.at[chunk, step],
            recv_sem=back_recv.at[chunk, step],
            device_id={"span": other},
            device_id_type=MESH,
        )

    def do_chunk(chunk, _):
        firsts = [half * share + chunk * part for half in range(2)]
        block = jnp.concatenate(
            [strided(across, first + p, total, owned) for first in firsts for p in range(part)],
            axis=0,
        )
        result = round_rows(layer_rows(block, group, bias, *inter_weights))
        size = part * total
        for half, first in enumerate(firsts):
            at = pl.multiple_of(first * total, size)
            for side in range(width // LANES):
                inter[side, pl.ds(at, size), :] = result[
                    half * size : (half + 1) * size, side * LANES : (side + 1) * LANES
                ]
        near = chunk * part * total
        far = (share + chunk * part) * total
        pieces = []
        for span in range(total):
            piece = strided(inter, near + span, part, total)
            if span > 0:
                piece = piece + strided(inter, far + span - 1, part, total)
            pieces.append(piece)
        back[chunk] = jnp.concatenate(pieces, axis=0).astype(jnp.bfloat16)
        for step in range(1, devices):
            send_back(chunk, step).start()
        size = spans * part
        got[chunk, me] = back[chunk, pl.ds(pl.multiple_of(me * size, TILE), size), :]
        return 0

    lax.fori_loop(0, chunks, do_chunk, 0)

    def collect(source):
        pieces = [
            got[chunk, source].astype(jnp.float32).reshape(spans, part, width)
            for chunk in range(chunks)
        ]
        summed = jnp.concatenate(pieces, axis=1).reshape(spans * share, width)
        mask = jnp.maximum(dot(summed.astype(jnp.bfloat16), w_mask[...]), 0.0)
        at = pl.multiple_of(source * share, TILE)
        enc = [frames[0, pl.ds(span * HOP + at, share), :] for span in range(spans)]
        enc = jnp.concatenate(enc, axis=0).astype(jnp.float32)
        out = mask * jnp.concatenate([enc] * SPK, axis=1)
        out = out.astype(jnp.bfloat16).reshape(spans, share, SPK * width)
        out_ref[:, pl.ds(at, share), :] = out

    collect(me)
    for step in range(1, devices):
        for chunk in range(chunks):
            send_back(chunk, step).wait_recv()
        collect(lax.rem(me + devices - step, devices))

    def drain_back(chunk, _):
        for step in range(1, devices):
            send_back(chunk, step).wait_send()
        return 0

    send_audio.wait_send()
    for section in range(2):
        send_halo(section).wait_send()
        for step in range(1, members):
            send_out(section, step).wait_send()
    lax.fori_loop(0, chunks, drain_back, 0)


def kernel_body(devices, audio, w_enc, *weights):
    width = w_enc.shape[1]
    rows = audio.shape[0] // LANES
    count = audio.shape[0] // STRIDE
    spans = count // HOP
    total = spans * devices
    share = HOP // devices
    chunks = 2
    part = share // chunks
    group = LANES
    operands = (
        audio.reshape(rows, LANES),
        w_enc,
        position_values(K, width),
        position_values(total, width),
        *weights,
    )
    vmem = pl.BlockSpec(memory_space=pltpu.VMEM)
    far = pl.BlockSpec(memory_space=pl.ANY)
    dma = pltpu.SemaphoreType.DMA
    separated = pl.pallas_call(
        functools.partial(separator_kernel, devices, group),
        out_shape=jax.ShapeDtypeStruct((spans, HOP, SPK * width), jnp.bfloat16),
        in_specs=[far] * len(operands),
        out_specs=vmem,
        scratch_shapes=[
            pltpu.VMEM((2, rows + 2 * HOP * STRIDE // LANES, LANES), jnp.float32),
            *[pltpu.VMEM(operand.shape, operand.dtype) for operand in operands[1:]],
            pltpu.VMEM((2, count + HOP, width), jnp.bfloat16),
            pltpu.VMEM((spans, K // HOP, HOP, width), jnp.bfloat16),
            pltpu.VMEM((2, spans, K // HOP, HOP // 2, width), jnp.bfloat16),
            pltpu.VMEM((total, K // HOP, share, width), jnp.bfloat16),
            pltpu.VMEM((width // LANES, total * 2 * share, LANES), jnp.float32),
            pltpu.VMEM((width // LANES, total * 2 * share, LANES), jnp.float32),
            pltpu.VMEM((chunks, total * part, width), jnp.bfloat16),
            pltpu.VMEM((chunks, devices, spans * part, width), jnp.bfloat16),
            dma,
            dma,
            dma((2,)),
            dma((2,)),
            dma((2, devices // 2)),
            dma((2, devices // 2)),
            dma((chunks, devices)),
            dma((chunks, devices)),
            dma((len(operands),)),
        ],
        compiler_params=pltpu.CompilerParams(
            collective_id=0, has_side_effects=True, vmem_limit_bytes=60 * 2**20
        ),
    )(*operands)
    return separated.reshape(count, SPK * width)


def fits_kernel(devices, count):
    spans = count // HOP
    share = HOP // devices
    return (
        HOP % devices == 0
        and share % TILE == 0
        and LANES % (spans * devices) == 0
        and share * (devices // 2) == HOP // 2
        and spans >= 4
        and spans % 2 == 0
        and devices % 2 == 0
    )


def body(audio, w_enc, *weights):
    devices = lax.axis_size("span")
    if fits_kernel(devices, audio.shape[0] // STRIDE):
        return kernel_body(devices, audio, w_enc, *weights)
    return plain_body(audio, w_enc, *weights)


def solution(mesh):
    placed = (P(("mix", "span")), P(), P(), P(), P(), P(), P(), P(), P(), P(), P(), P(), P())
    return jax.shard_map(
        body, mesh=mesh, in_specs=placed, out_specs=P(("mix", "span"), None), check_vma=False
    )
```

```python
import functools
import math

import jax
import jax.numpy as jnp
import numpy as np
from jax import lax
from jax.experimental import pallas as pl
from jax.experimental.pallas import tpu as pltpu
from jax.sharding import PartitionSpec as P

HEADS = 8
K = 256
HOP = 128
STRIDE = 8
SPK = 2


def shifted_2(block, axis, distance):
    devices = range(lax.axis_size(axis))
    route = [(i - distance, i) for i in devices if i - distance in devices]
    return lax.ppermute(block, axis, route)


def norm_rows(values):
    center = values - jnp.mean(values, axis=-1, keepdims=True)
    spread = jnp.mean(center * center, axis=-1, keepdims=True)
    return center * lax.rsqrt(spread + 1e-05)


def positions_table(count, width):
    place = jnp.arange(count, dtype=jnp.float32)[:, None]
    index = jnp.arange(width // 2, dtype=jnp.float32)[None, :]
    angle = place * jnp.exp(-math.log(10000.0) * 2.0 * index / width)
    return jnp.concatenate([jnp.sin(angle), jnp.cos(angle)], axis=1)


def matmul(rows, weight):
    shape = rows.shape
    flat = rows.reshape(-1, shape[-1])
    result = jnp.dot(flat, weight, preferred_element_type=jnp.float32)
    return result.reshape(shape[:-1] + (weight.shape[1],))


def attend_block(items):
    query_vectors, key_matrix_rows, value_matrix_rows = items
    score_scale = 1.0 / math.sqrt(query_vectors.shape[-1])
    logit_scores = (
        jnp.einsum(
            "blhd,bmhd->bhlm", query_vectors, key_matrix_rows, preferred_element_type=jnp.float32
        )
        * score_scale
    )
    logit_scores = logit_scores - jnp.max(logit_scores, axis=-1, keepdims=True)
    softmax_weights = jnp.exp(logit_scores)
    softmax_weights = (softmax_weights / jnp.sum(softmax_weights, axis=-1, keepdims=True)).astype(
        jnp.bfloat16
    )
    return jnp.einsum(
        "bhlm,bmhd->blhd", softmax_weights, value_matrix_rows, preferred_element_type=jnp.float32
    ).astype(jnp.bfloat16)


def layer(inputs, w_query, w_kv, w_out, w_up, w_down):
    batch, length, width = inputs.shape
    depth = width // HEADS
    group = math.gcd(batch, max(1, 1024 // length))
    blocks = batch // group
    normed = norm_rows(inputs.astype(jnp.float32)).astype(jnp.bfloat16)
    query_vectors = (
        matmul(normed, w_query).astype(jnp.bfloat16).reshape(blocks, group, length, HEADS, depth)
    )
    pair = matmul(normed, w_kv).astype(jnp.bfloat16)
    key_matrix_rows = pair[..., :width].reshape(blocks, group, length, HEADS, depth)
    value_matrix_rows = pair[..., width:].reshape(blocks, group, length, HEADS, depth)
    mixed = lax.map(attend_block, (query_vectors, key_matrix_rows, value_matrix_rows)).reshape(
        batch, length, width
    )
    middle_value = (inputs.astype(jnp.float32) + matmul(mixed, w_out)).astype(jnp.bfloat16)
    second_operand = norm_rows(middle_value.astype(jnp.float32)).astype(jnp.bfloat16)
    hidden = jax.nn.relu(matmul(second_operand, w_up)).astype(jnp.bfloat16)
    return (middle_value.astype(jnp.float32) + matmul(hidden, w_down)).astype(jnp.bfloat16)


def encode_rows(samples, w_enc):
    blocks = samples.reshape(-1, STRIDE)
    frames = jnp.concatenate([blocks[:-1], blocks[1:]], axis=1)
    result = jnp.dot(
        frames, w_enc, precision=lax.Precision.HIGHEST, preferred_element_type=jnp.float32
    )
    return jax.nn.relu(result).astype(jnp.bfloat16)


def plain_body(
    audio,
    w_enc,
    intra_query,
    intra_kv,
    intra_out,
    intra_up,
    intra_down,
    inter_query,
    inter_kv,
    inter_out,
    inter_up,
    inter_down,
    w_mask,
):
    frame_count = audio.shape[0] // STRIDE
    width = w_enc.shape[1]
    local_spans = frame_count // HOP
    devices = lax.axis_size("span")
    extra = shifted_2(audio[: (HOP + 1) * STRIDE], "span", -1)
    padded = encode_rows(jnp.concatenate([audio, extra], axis=0), w_enc)
    enc = padded[:frame_count]
    spans = jnp.concatenate(
        [
            padded[:frame_count].reshape(local_spans, HOP, width),
            padded[HOP:].reshape(local_spans, HOP, width),
        ],
        axis=1,
    )
    start = (spans.astype(jnp.float32) + positions_table(K, width)[None]).astype(jnp.bfloat16)
    intra = layer(start, intra_query, intra_kv, intra_out, intra_up, intra_down)
    per_device = K // devices
    grouped = intra.reshape(local_spans, devices, per_device, width)
    gathered = lax.all_to_all(grouped, "span", split_axis=1, concat_axis=0, tiled=True)
    total = gathered.shape[0]
    plain = gathered[:, 0]
    shifted = (plain.astype(jnp.float32) + positions_table(total, width)[:, None, :]).astype(
        jnp.bfloat16
    )
    turned = jnp.transpose(shifted, (1, 0, 2))
    result = layer(turned, inter_query, inter_kv, inter_out, inter_up, inter_down)
    inter = jnp.transpose(result, (1, 0, 2))[:, None]
    back = lax.all_to_all(inter, "span", split_axis=0, concat_axis=1, tiled=True).reshape(
        local_spans, K, width
    )
    second_half = back[:, HOP:]
    carried = shifted_2(second_half[-1], "span", 1)
    earlier = jnp.concatenate([carried[None], second_half[:-1]], axis=0)
    summed = back[:, :HOP].astype(jnp.float32) + earlier.astype(jnp.float32)
    summed = summed.reshape(frame_count, width).astype(jnp.bfloat16)
    mask = jax.nn.relu(jnp.dot(summed, w_mask, preferred_element_type=jnp.float32))
    repeated = jnp.concatenate([enc] * SPK, axis=1).astype(jnp.float32)
    return (mask * repeated).astype(jnp.bfloat16)


LANES = 128
TILE = 16
OPERANDS = 15
MESH = pl.DeviceIdType.MESH


def position_values(count, width):
    place = np.arange(count, dtype=np.float64)[:, None]
    index = np.arange(width // 2, dtype=np.float64)[None, :]
    angle = place * np.exp(-math.log(10000.0) * 2.0 * index / width)
    return np.concatenate([np.sin(angle), np.cos(angle)], axis=1).astype(np.float32)


def dot(left, right):
    return jnp.dot(left, right, preferred_element_type=jnp.float32)


def round_rows(values):
    return values.astype(jnp.bfloat16).astype(jnp.float32)


def strided(ref, first, count, stride):
    picked = [ref[side, pl.ds(first, count, stride=stride), :] for side in range(ref.shape[0])]
    return jnp.concatenate(picked, axis=1)


def attend_rows(query, key, value, bias):
    rows, width = query.shape
    depth = width // HEADS
    owner = lax.broadcasted_iota(jnp.int32, (1, LANES), 1) // depth
    zero = jnp.zeros((), jnp.bfloat16)
    ones = jnp.ones((key.shape[0], LANES), jnp.bfloat16)
    heads = LANES // depth
    sides = []
    for at in range(0, width, LANES):
        side_query, side_key, side_value = (
            block[:, at : at + LANES] for block in (query, key, value)
        )
        scores = lax.dot_general(
            jnp.concatenate(
                [jnp.where(owner == head, side_query, zero) for head in range(heads)], axis=0
            ),
            side_key,
            (((1,), (1,)), ((), ())),
            preferred_element_type=jnp.float32,
        )
        if bias is not None:
            scores = scores + jnp.concatenate([bias] * heads, axis=0)
        scores = scores - jnp.max(scores, axis=-1, keepdims=True)
        weights = jnp.exp2(scores.astype(jnp.bfloat16))
        result = dot(weights, jnp.concatenate([side_value, ones], axis=1))
        owners = jnp.concatenate([owner, owner], axis=1)
        total = result[:rows]
        for head in range(1, heads):
            total = jnp.where(owners == head, result[head * rows : (head + 1) * rows], total)
        sides.append(total[:, :LANES] / total[:, LANES:])
    return jnp.concatenate(sides, axis=1).astype(jnp.bfloat16)


def query_rows(normed, w_query):
    scale = math.log2(math.e) / math.sqrt(normed.shape[1] // HEADS)
    return (dot(normed, w_query[...]) * scale).astype(jnp.bfloat16)


def rest_rows(rows, mixed, w_out, w_up, w_down):
    middle = round_rows(rows + dot(mixed, w_out[...]))
    second = norm_rows(middle).astype(jnp.bfloat16)
    hidden = jnp.maximum(dot(second, w_up[...]), 0.0).astype(jnp.bfloat16)
    return middle + dot(hidden, w_down[...])


def separator_kernel(devices, group, *refs):
    given, refs = refs[:OPERANDS], refs[OPERANDS:]
    out_ref, refs = refs[0], refs[1:]
    held, refs = refs[:OPERANDS], refs[OPERANDS:]
    audio = given[0]
    samples, w_enc, table_span, table_across, *layers = held
    intra_query, intra_kv, *intra_rest = layers[:5]
    inter_weights = layers[5:10]
    w_mask = layers[10]
    (
        frames,
        normed,
        started,
        mixed,
        queries,
        pairs,
        sent,
        taken,
        across,
        inter,
        back,
        got,
        audio_send,
        audio_recv,
        halo_send,
        halo_recv,
        out_send,
        out_recv,
        back_send,
        back_recv,
        load,
    ) = refs
    me = lax.axis_index("span")
    width = w_enc.shape[1]
    rows = audio.shape[0]
    per_row = LANES // STRIDE
    count = rows * per_row
    spans = count // HOP
    share = HOP // devices
    owned = 2 * share
    total = spans * devices
    chunks = back.shape[0]
    part = share // chunks
    members = devices // 2
    half_hop = HOP // 2
    halo_rows = samples.shape[1] - rows
    partner = lax.rem(me + members, devices)
    group_at = me // members
    member = lax.rem(me, members)

    loads = []
    for index in range(OPERANDS):
        target = samples.at[0, pl.ds(0, rows)] if index == 0 else held[index]
        loads.append(pltpu.make_async_copy(given[index], target, load.at[index]))
    for index in range(9):
        loads[index].start()

    barrier = pltpu.get_barrier_semaphore()
    for step in range(1, devices):
        other = lax.rem(me + step, devices)
        pl.semaphore_signal(barrier, inc=1, device_id={"span": other}, device_id_type=MESH)

    def send_halo(section):
        other = lax.rem(me + devices - 1 + section * members, devices)
        return pltpu.make_async_remote_copy(
            src_ref=audio.at[pl.ds(0, halo_rows)],
            dst_ref=samples.at[section, pl.ds(rows, halo_rows)],
            send_sem=halo_send.at[section],
            recv_sem=halo_recv.at[section],
            device_id={"span": other},
            device_id_type=MESH,
        )

    send_audio = pltpu.make_async_remote_copy(
        src_ref=audio,
        dst_ref=samples.at[1, pl.ds(0, rows)],
        send_sem=audio_send,
        recv_sem=audio_recv,
        device_id={"span": partner},
        device_id_type=MESH,
    )

    lane = lax.broadcasted_iota(jnp.int32, (1, LANES), 1)
    slot = lax.broadcasted_iota(jnp.int32, (HOP, 1), 0) % per_row
    mine = lane // STRIDE == slot
    for index in range(4):
        loads[index].wait()
    w_low = jnp.concatenate([w_enc[:STRIDE]] * per_row, axis=0)
    w_high = jnp.concatenate([w_enc[STRIDE:]] * per_row, axis=0)
    w_both = jnp.concatenate([w_low, w_high], axis=0)
    w_lead = w_both.astype(jnp.bfloat16)
    w_rest = (w_both - w_lead.astype(jnp.float32)).astype(jnp.bfloat16)
    step_rows = HOP // per_row
    kind = [lax.broadcasted_iota(jnp.int32, (group, group), axis) // total for axis in (0, 1)]
    bias = jnp.where(kind[0] == kind[1], 0.0, -1e30)

    def encode(section, hop):
        at = pl.multiple_of(hop * step_rows, step_rows)
        low = samples[section, pl.ds(at, step_rows), :]
        turned = pltpu.roll(samples[section, pl.ds(at, 2 * step_rows), :], LANES - STRIDE, 1)
        high = jnp.where(lane < LANES - STRIDE, turned[:step_rows], turned[1 : step_rows + 1])
        leads = []
        rests = []
        for block in (low, high):
            lead = block.astype(jnp.bfloat16).astype(jnp.float32)
            for values, into in ((lead, leads), (block - lead, rests)):
                spread = jnp.concatenate(
                    [
                        jnp.broadcast_to(values[r : r + 1], (per_row, LANES))
                        for r in range(step_rows)
                    ],
                    axis=0,
                )
                into.append(jnp.where(mine, spread, 0.0).astype(jnp.bfloat16))
        lead = jnp.concatenate(leads, axis=1)
        rest = jnp.concatenate(rests, axis=1)
        result = dot(lead, w_lead) + (dot(rest, w_lead) + dot(lead, w_rest))
        at = pl.multiple_of(hop * HOP, HOP)
        frames[section, pl.ds(at, HOP), :] = jnp.maximum(result, 0.0).astype(jnp.bfloat16)

    def encode_all(section, first, last):
        lax.fori_loop(first, last, lambda hop, _: (encode(section, hop), 0)[1], 0)

    encode_all(0, 0, spans - 1)
    pl.semaphore_wait(barrier, devices - 1)
    send_halo(0).start()
    send_audio.start()
    send_halo(1).start()
    for index in range(4, 9):
        loads[index].wait()
    for index in range(9, OPERANDS):
        loads[index].start()
    near = pl.multiple_of(group_at * half_hop, half_hop)

    def send_out(section, step):
        other = lax.rem(member + step, members)
        source = lax.rem(me + section * members, devices)
        return pltpu.make_async_remote_copy(
            src_ref=sent.at[section, :, :, pl.ds(pl.multiple_of(other * share, TILE), share), :],
            dst_ref=taken.at[pl.ds(source * spans, spans)],
            send_sem=out_send.at[section, step],
            recv_sem=out_recv.at[section, step],
            device_id={"span": group_at * members + other},
            device_id_type=MESH,
        )

    def do_section(section, _):
        source = lax.rem(me + section * members, devices)

        @pl.when(section == 1)
        def _():
            send_audio.wait_recv()

        send_halo(section).wait_recv()

        @pl.when(source == devices - 1)
        def _():
            samples[section, rows:] = jnp.zeros((halo_rows, LANES), jnp.float32)

        encode_all(section, (spans - 1) * (1 - section), spans + 1)

        def do_span(index, _):
            at = pl.multiple_of(index * HOP, HOP)
            start = frames[section, pl.ds(at, K), :].astype(jnp.float32)
            start = round_rows(start + table_span[...])
            values = norm_rows(start).astype(jnp.bfloat16)
            normed[...] = values.reshape(K // HOP, HOP, width)
            for half in range(K // HOP):
                at = pl.multiple_of(index * HOP + half * HOP + near, half_hop)
                start = frames[section, pl.ds(at, half_hop), :].astype(jnp.float32)
                at = pl.multiple_of(half * HOP + near, half_hop)
                start = round_rows(start + table_span[pl.ds(at, half_hop), :])
                at = pl.multiple_of(index * HOP + half * half_hop, half_hop)
                started[pl.ds(at, half_hop), :] = start
            pair = dot(values, intra_kv[...]).astype(jnp.bfloat16)
            mine_normed = normed[:, pl.ds(near, half_hop), :].reshape(HOP, width)
            query = query_rows(mine_normed, intra_query)
            at = pl.multiple_of(index * HOP, HOP)
            mixed[pl.ds(at, HOP), :] = attend_rows(query, pair[:, :width], pair[:, width:], None)
            return 0

        lax.fori_loop(0, spans, do_span, 0)
        result = rest_rows(started[...], mixed[...], *intra_rest)
        result = result.astype(jnp.bfloat16)
        sent[section] = result.reshape(spans, K // HOP, half_hop, width)
        for step in range(1, members):
            send_out(section, step).start()
        at = pl.multiple_of(member * share, TILE)
        taken[pl.ds(source * spans, spans)] = sent[section, :, :, pl.ds(at, share), :]
        return 0

    lax.fori_loop(0, 2, do_section, 0)

    for index in range(9, OPERANDS):
        loads[index].wait()

    def place(source):
        def place_one(index, _):
            row = source * spans + index
            block = taken[row].reshape(owned, width).astype(jnp.float32)
            at = pl.multiple_of(row * owned, owned)
            block = round_rows(block + table_across[pl.ds(row, 1), :])
            for side in range(width // LANES):
                across[side, pl.ds(at, owned), :] = block[:, side * LANES : (side + 1) * LANES]
            return 0

        lax.fori_loop(0, spans, place_one, 0)

    def place_section(section, _):
        place(lax.rem(me + section * members, devices))
        for step in range(1, members):
            send_out(section, step).wait_recv()
            other = group_at * members + lax.rem(member + members - step, members)
            place(lax.rem(other + section * members, devices))
        return 0

    lax.fori_loop(0, 2, place_section, 0)

    def send_back(chunk, step):
        other = lax.rem(me + step, devices)
        size = spans * part
        return pltpu.make_async_remote_copy(
            src_ref=back.at[chunk, pl.ds(pl.multiple_of(other * size, TILE), size), :],
            dst_ref=got.at[chunk, me],
            send_sem=back_send.at[chunk, step],
            recv_sem=back_recv.at[chunk, step],
            device_id={"span": other},
            device_id_type=MESH,
        )

    def do_chunk(chunk, _):
        firsts = [half * share + chunk * part for half in range(2)]
        block = jnp.concatenate(
            [strided(across, first + p, total, owned) for first in firsts for p in range(part)],
            axis=0,
        )
        inter_query, inter_kv, *inter_rest = inter_weights
        values = norm_rows(block).astype(jnp.bfloat16)
        queries[...] = query_rows(values, inter_query)
        pairs[...] = dot(values, inter_kv[...]).astype(jnp.bfloat16)

        def do_group(index, _):
            at = pl.ds(pl.multiple_of(index * group, group), group)
            mixed[at, :] = attend_rows(
                queries[at, :], pairs[at, :width], pairs[at, width:], bias
            )
            return 0

        lax.fori_loop(0, 2 * part * total // group, do_group, 0)
        result = round_rows(rest_rows(block, mixed[...], *inter_rest))
        size = part * total
        for half, first in enumerate(firsts):
            at = pl.multiple_of(first * total, size)
            for side in range(width // LANES):
                inter[side, pl.ds(at, size), :] = result[
                    half * size : (half + 1) * size, side * LANES : (side + 1) * LANES
                ]
        near = chunk * part * total
        far = (share + chunk * part) * total
        pieces = []
        for span in range(total):
            piece = strided(inter, near + span, part, total)
            if span > 0:
                piece = piece + strided(inter, far + span - 1, part, total)
            pieces.append(piece)
        back[chunk] = jnp.concatenate(pieces, axis=0).astype(jnp.bfloat16)
        for step in range(1, devices):
            send_back(chunk, step).start()
        size = spans * part
        got[chunk, me] = back[chunk, pl.ds(pl.multiple_of(me * size, TILE), size), :]
        return 0

    lax.fori_loop(0, chunks, do_chunk, 0)

    def collect(source):
        pieces = [
            got[chunk, source].astype(jnp.float32).reshape(spans, part, width)
            for chunk in range(chunks)
        ]
        summed = jnp.concatenate(pieces, axis=1).reshape(spans * share, width)
        mask = jnp.maximum(dot(summed.astype(jnp.bfloat16), w_mask[...]), 0.0)
        at = pl.multiple_of(source * share, TILE)
        enc = [frames[0, pl.ds(span * HOP + at, share), :] for span in range(spans)]
        enc = jnp.concatenate(enc, axis=0).astype(jnp.float32)
        out = mask * jnp.concatenate([enc] * SPK, axis=1)
        out = out.astype(jnp.bfloat16).reshape(spans, share, SPK * width)
        out_ref[:, pl.ds(at, share), :] = out

    collect(me)

    def collect_step(step, _):
        for chunk in range(chunks):
            send_back(chunk, step).wait_recv()
        collect(lax.rem(me + devices - step, devices))
        return 0

    lax.fori_loop(1, devices, collect_step, 0)

    def drain_back(chunk, _):
        for step in range(1, devices):
            send_back(chunk, step).wait_send()
        return 0

    send_audio.wait_send()
    for section in range(2):
        send_halo(section).wait_send()
        for step in range(1, members):
            send_out(section, step).wait_send()
    lax.fori_loop(0, chunks, drain_back, 0)


def kernel_body(devices, audio, w_enc, *weights):
    width = w_enc.shape[1]
    rows = audio.shape[0] // LANES
    count = audio.shape[0] // STRIDE
    spans = count // HOP
    total = spans * devices
    share = HOP // devices
    chunks = 2
    part = share // chunks
    group = LANES
    operands = (
        audio.reshape(rows, LANES),
        w_enc,
        position_values(K, width),
        position_values(total, width),
        *weights,
    )
    vmem = pl.BlockSpec(memory_space=pltpu.VMEM)
    far = pl.BlockSpec(memory_space=pl.ANY)
    dma = pltpu.SemaphoreType.DMA
    separated = pl.pallas_call(
        functools.partial(separator_kernel, devices, group),
        out_shape=jax.ShapeDtypeStruct((spans, HOP, SPK * width), jnp.bfloat16),
        in_specs=[far] * len(operands),
        out_specs=vmem,
        scratch_shapes=[
            pltpu.VMEM((2, rows + 2 * HOP * STRIDE // LANES, LANES), jnp.float32),
            *[pltpu.VMEM(operand.shape, operand.dtype) for operand in operands[1:]],
            pltpu.VMEM((2, count + HOP, width), jnp.bfloat16),
            pltpu.VMEM((K // HOP, HOP, width), jnp.bfloat16),
            pltpu.VMEM((count, width), jnp.float32),
            pltpu.VMEM((count, width), jnp.bfloat16),
            pltpu.VMEM((count, width), jnp.bfloat16),
            pltpu.VMEM((count, 2 * width), jnp.bfloat16),
            pltpu.VMEM((2, spans, K // HOP, HOP // 2, width), jnp.bfloat16),
            pltpu.VMEM((total, K // HOP, share, width), jnp.bfloat16),
            pltpu.VMEM((width // LANES, total * 2 * share, LANES), jnp.float32),
            pltpu.VMEM((width // LANES, total * 2 * share, LANES), jnp.float32),
            pltpu.VMEM((chunks, total * part, width), jnp.bfloat16),
            pltpu.VMEM((chunks, devices, spans * part, width), jnp.bfloat16),
            dma,
            dma,
            dma((2,)),
            dma((2,)),
            dma((2, devices // 2)),
            dma((2, devices // 2)),
            dma((chunks, devices)),
            dma((chunks, devices)),
            dma((len(operands),)),
        ],
        compiler_params=pltpu.CompilerParams(
            collective_id=0, has_side_effects=True, vmem_limit_bytes=60 * 2**20
        ),
    )(*operands)
    return separated.reshape(count, SPK * width)


def fits_kernel(devices, count):
    spans = count // HOP
    share = HOP // devices
    return (
        HOP % devices == 0
        and share % TILE == 0
        and LANES % (spans * devices) == 0
        and spans >= 4
        and spans % 2 == 0
        and devices % 2 == 0
    )


def body(audio, w_enc, *weights):
    devices = lax.axis_size("span")
    if fits_kernel(devices, audio.shape[0] // STRIDE):
        return kernel_body(devices, audio, w_enc, *weights)
    return plain_body(audio, w_enc, *weights)


def solution(mesh):
    placed = (P(("mix", "span")), P(), P(), P(), P(), P(), P(), P(), P(), P(), P(), P(), P())
    return jax.shard_map(
        body, mesh=mesh, in_specs=placed, out_specs=P(("mix", "span"), None), check_vma=False
    )
```

```python
import functools
import math

import jax
import jax.numpy as jnp
import numpy as np
from jax import lax
from jax.experimental import pallas as pl
from jax.experimental.pallas import tpu as pltpu
from jax.sharding import PartitionSpec as P

HEADS = 8
K = 256
HOP = 128
STRIDE = 8
SPK = 2


def shifted_2(block, axis, distance):
    devices = range(lax.axis_size(axis))
    route = [(i - distance, i) for i in devices if i - distance in devices]
    return lax.ppermute(block, axis, route)


def norm_rows(values):
    center = values - jnp.mean(values, axis=-1, keepdims=True)
    spread = jnp.mean(center * center, axis=-1, keepdims=True)
    return center * lax.rsqrt(spread + 1e-05)


def positions_table(count, width):
    place = jnp.arange(count, dtype=jnp.float32)[:, None]
    index = jnp.arange(width // 2, dtype=jnp.float32)[None, :]
    angle = place * jnp.exp(-math.log(10000.0) * 2.0 * index / width)
    return jnp.concatenate([jnp.sin(angle), jnp.cos(angle)], axis=1)


def matmul(rows, weight):
    shape = rows.shape
    flat = rows.reshape(-1, shape[-1])
    result = jnp.dot(flat, weight, preferred_element_type=jnp.float32)
    return result.reshape(shape[:-1] + (weight.shape[1],))


def attend_block(items):
    query_vectors, key_matrix_rows, value_matrix_rows = items
    score_scale = 1.0 / math.sqrt(query_vectors.shape[-1])
    logit_scores = (
        jnp.einsum(
            "blhd,bmhd->bhlm", query_vectors, key_matrix_rows, preferred_element_type=jnp.float32
        )
        * score_scale
    )
    logit_scores = logit_scores - jnp.max(logit_scores, axis=-1, keepdims=True)
    softmax_weights = jnp.exp(logit_scores)
    softmax_weights = (softmax_weights / jnp.sum(softmax_weights, axis=-1, keepdims=True)).astype(
        jnp.bfloat16
    )
    return jnp.einsum(
        "bhlm,bmhd->blhd", softmax_weights, value_matrix_rows, preferred_element_type=jnp.float32
    ).astype(jnp.bfloat16)


def layer(inputs, w_query, w_kv, w_out, w_up, w_down):
    batch, length, width = inputs.shape
    depth = width // HEADS
    group = math.gcd(batch, max(1, 1024 // length))
    blocks = batch // group
    normed = norm_rows(inputs.astype(jnp.float32)).astype(jnp.bfloat16)
    query_vectors = (
        matmul(normed, w_query).astype(jnp.bfloat16).reshape(blocks, group, length, HEADS, depth)
    )
    pair = matmul(normed, w_kv).astype(jnp.bfloat16)
    key_matrix_rows = pair[..., :width].reshape(blocks, group, length, HEADS, depth)
    value_matrix_rows = pair[..., width:].reshape(blocks, group, length, HEADS, depth)
    mixed = lax.map(attend_block, (query_vectors, key_matrix_rows, value_matrix_rows)).reshape(
        batch, length, width
    )
    middle_value = (inputs.astype(jnp.float32) + matmul(mixed, w_out)).astype(jnp.bfloat16)
    second_operand = norm_rows(middle_value.astype(jnp.float32)).astype(jnp.bfloat16)
    hidden = jax.nn.relu(matmul(second_operand, w_up)).astype(jnp.bfloat16)
    return (middle_value.astype(jnp.float32) + matmul(hidden, w_down)).astype(jnp.bfloat16)


def encode_rows(samples, w_enc):
    blocks = samples.reshape(-1, STRIDE)
    frames = jnp.concatenate([blocks[:-1], blocks[1:]], axis=1)
    result = jnp.dot(
        frames, w_enc, precision=lax.Precision.HIGHEST, preferred_element_type=jnp.float32
    )
    return jax.nn.relu(result).astype(jnp.bfloat16)


def plain_body(
    audio,
    w_enc,
    intra_query,
    intra_kv,
    intra_out,
    intra_up,
    intra_down,
    inter_query,
    inter_kv,
    inter_out,
    inter_up,
    inter_down,
    w_mask,
):
    frame_count = audio.shape[0] // STRIDE
    width = w_enc.shape[1]
    local_spans = frame_count // HOP
    devices = lax.axis_size("span")
    extra = shifted_2(audio[: (HOP + 1) * STRIDE], "span", -1)
    padded = encode_rows(jnp.concatenate([audio, extra], axis=0), w_enc)
    enc = padded[:frame_count]
    spans = jnp.concatenate(
        [
            padded[:frame_count].reshape(local_spans, HOP, width),
            padded[HOP:].reshape(local_spans, HOP, width),
        ],
        axis=1,
    )
    start = (spans.astype(jnp.float32) + positions_table(K, width)[None]).astype(jnp.bfloat16)
    intra = layer(start, intra_query, intra_kv, intra_out, intra_up, intra_down)
    per_device = K // devices
    grouped = intra.reshape(local_spans, devices, per_device, width)
    gathered = lax.all_to_all(grouped, "span", split_axis=1, concat_axis=0, tiled=True)
    total = gathered.shape[0]
    plain = gathered[:, 0]
    shifted = (plain.astype(jnp.float32) + positions_table(total, width)[:, None, :]).astype(
        jnp.bfloat16
    )
    turned = jnp.transpose(shifted, (1, 0, 2))
    result = layer(turned, inter_query, inter_kv, inter_out, inter_up, inter_down)
    inter = jnp.transpose(result, (1, 0, 2))[:, None]
    back = lax.all_to_all(inter, "span", split_axis=0, concat_axis=1, tiled=True).reshape(
        local_spans, K, width
    )
    second_half = back[:, HOP:]
    carried = shifted_2(second_half[-1], "span", 1)
    earlier = jnp.concatenate([carried[None], second_half[:-1]], axis=0)
    summed = back[:, :HOP].astype(jnp.float32) + earlier.astype(jnp.float32)
    summed = summed.reshape(frame_count, width).astype(jnp.bfloat16)
    mask = jax.nn.relu(jnp.dot(summed, w_mask, preferred_element_type=jnp.float32))
    repeated = jnp.concatenate([enc] * SPK, axis=1).astype(jnp.float32)
    return (mask * repeated).astype(jnp.bfloat16)


LANES = 128
TILE = 16
OPERANDS = 15
MESH = pl.DeviceIdType.MESH


def aligned(value, unit):
    return value if isinstance(value, int) else pl.multiple_of(value, unit)


def position_values(count, width):
    place = np.arange(count, dtype=np.float64)[:, None]
    index = np.arange(width // 2, dtype=np.float64)[None, :]
    angle = place * np.exp(-math.log(10000.0) * 2.0 * index / width)
    return np.concatenate([np.sin(angle), np.cos(angle)], axis=1).astype(np.float32)


def dot(left, right):
    return jnp.dot(left, right, preferred_element_type=jnp.float32)


def norm_wide(rows):
    width = rows.shape[1]
    ones = jnp.ones((width, LANES), jnp.bfloat16)
    mean = dot(rows.astype(jnp.bfloat16), ones) * (1.0 / width)
    center = [rows[:, at : at + LANES] - mean for at in range(0, width, LANES)]
    squares = jnp.concatenate([(part * part).astype(jnp.bfloat16) for part in center], axis=1)
    scale = lax.rsqrt(dot(squares, ones) * (1.0 / width) + 1e-05)
    return jnp.concatenate([part * scale for part in center], axis=1)


def round_rows(values):
    return values.astype(jnp.bfloat16).astype(jnp.float32)


def strided(ref, first, count, stride):
    picked = [ref[side, pl.ds(first, count, stride=stride), :] for side in range(ref.shape[0])]
    return jnp.concatenate(picked, axis=1)


def attend_rows(query, key, value, bias):
    rows, width = query.shape
    depth = width // HEADS
    owner = lax.broadcasted_iota(jnp.int32, (1, LANES), 1) // depth
    zero = jnp.zeros((), jnp.bfloat16)
    ones = jnp.ones((key.shape[0], LANES), jnp.bfloat16)
    heads = LANES // depth
    sides = []
    for at in range(0, width, LANES):
        side_query, side_key, side_value = (
            block[:, at : at + LANES] for block in (query, key, value)
        )
        scores = lax.dot_general(
            jnp.concatenate(
                [jnp.where(owner == head, side_query, zero) for head in range(heads)], axis=0
            ),
            side_key,
            (((1,), (1,)), ((), ())),
            preferred_element_type=jnp.float32,
        )
        if bias is not None:
            scores = scores + jnp.concatenate([bias] * heads, axis=0)
        scores = scores - jnp.max(scores, axis=-1, keepdims=True)
        weights = jnp.exp2(scores.astype(jnp.bfloat16))
        result = dot(weights, jnp.concatenate([side_value, ones], axis=1))
        owners = jnp.concatenate([owner, owner], axis=1)
        total = result[:rows]
        for head in range(1, heads):
            total = jnp.where(owners == head, result[head * rows : (head + 1) * rows], total)
        sides.append(total[:, :LANES] / total[:, LANES:])
    return jnp.concatenate(sides, axis=1).astype(jnp.bfloat16)


def query_rows(normed, w_query):
    scale = math.log2(math.e) / math.sqrt(normed.shape[1] // HEADS)
    return (dot(normed, w_query[...]) * scale).astype(jnp.bfloat16)


def rest_rows(rows, mixed, w_out, w_up, w_down):
    middle = round_rows(rows + dot(mixed, w_out[...]))
    second = norm_wide(middle).astype(jnp.bfloat16)
    hidden = jnp.maximum(dot(second, w_up[...]), 0.0).astype(jnp.bfloat16)
    return middle + dot(hidden, w_down[...])


def layer_rows(rows, group, bias, w_query, w_kv, w_out, w_up, w_down):
    width = rows.shape[1]
    normed = norm_wide(rows).astype(jnp.bfloat16)
    query = query_rows(normed, w_query)
    pair = dot(normed, w_kv[...]).astype(jnp.bfloat16)
    mixed = [
        attend_rows(
            query[at : at + group],
            pair[at : at + group, :width],
            pair[at : at + group, width:],
            bias,
        )
        for at in range(0, rows.shape[0], group)
    ]
    return rest_rows(rows, jnp.concatenate(mixed, axis=0), w_out, w_up, w_down)


def separator_kernel(devices, group, *refs):
    given, refs = refs[:OPERANDS], refs[OPERANDS:]
    out_ref, refs = refs[0], refs[1:]
    held, refs = refs[:OPERANDS], refs[OPERANDS:]
    audio = given[0]
    samples, w_enc, table_span, table_across, *layers = held
    intra_query, intra_kv, *intra_rest = layers[:5]
    inter_weights = layers[5:10]
    w_mask = layers[10]
    (
        frames,
        normed,
        sent,
        taken,
        across,
        inter,
        back,
        got,
        audio_send,
        audio_recv,
        halo_send,
        halo_recv,
        out_send,
        out_recv,
        back_send,
        back_recv,
        load,
    ) = refs
    me = lax.axis_index("span")
    width = w_enc.shape[1]
    rows = audio.shape[0]
    per_row = LANES // STRIDE
    count = rows * per_row
    spans = count // HOP
    share = HOP // devices
    owned = 2 * share
    total = spans * devices
    chunks = back.shape[0]
    part = share // chunks
    members = devices // 2
    half_hop = HOP // 2
    halo_rows = samples.shape[1] - rows
    partner = lax.rem(me + members, devices)
    group_at = me // members
    member = lax.rem(me, members)

    loads = []
    for index in range(OPERANDS):
        target = samples.at[0, pl.ds(0, rows)] if index == 0 else held[index]
        loads.append(pltpu.make_async_copy(given[index], target, load.at[index]))
    for index in range(9):
        loads[index].start()

    barrier = pltpu.get_barrier_semaphore()
    for step in range(1, devices):
        other = lax.rem(me + step, devices)
        pl.semaphore_signal(barrier, inc=1, device_id={"span": other}, device_id_type=MESH)

    def send_halo(section):
        other = lax.rem(me + devices - 1 + section * members, devices)
        return pltpu.make_async_remote_copy(
            src_ref=audio.at[pl.ds(0, halo_rows)],
            dst_ref=samples.at[section, pl.ds(rows, halo_rows)],
            send_sem=halo_send.at[section],
            recv_sem=halo_recv.at[section],
            device_id={"span": other},
            device_id_type=MESH,
        )

    send_audio = pltpu.make_async_remote_copy(
        src_ref=audio,
        dst_ref=samples.at[1, pl.ds(0, rows)],
        send_sem=audio_send,
        recv_sem=audio_recv,
        device_id={"span": partner},
        device_id_type=MESH,
    )

    lane = lax.broadcasted_iota(jnp.int32, (1, LANES), 1)
    slot = lax.broadcasted_iota(jnp.int32, (HOP, 1), 0) % per_row
    mine = lane // STRIDE == slot
    for index in range(4):
        loads[index].wait()
    w_low = jnp.concatenate([w_enc[:STRIDE]] * per_row, axis=0)
    w_high = jnp.concatenate([w_enc[STRIDE:]] * per_row, axis=0)
    w_both = jnp.concatenate([w_low, w_high], axis=0)
    w_lead = w_both.astype(jnp.bfloat16)
    w_rest = (w_both - w_lead.astype(jnp.float32)).astype(jnp.bfloat16)
    step_rows = HOP // per_row
    kind = [lax.broadcasted_iota(jnp.int32, (group, group), axis) // total for axis in (0, 1)]
    bias = jnp.where(kind[0] == kind[1], 0.0, -1e30)

    def encode(section, hop):
        at = hop * step_rows
        low = samples[section, pl.ds(at, step_rows), :]
        turned = pltpu.roll(samples[section, pl.ds(at, 2 * step_rows), :], LANES - STRIDE, 1)
        high = jnp.where(lane < LANES - STRIDE, turned[:step_rows], turned[1 : step_rows + 1])
        leads = []
        rests = []
        for block in (low, high):
            lead = block.astype(jnp.bfloat16).astype(jnp.float32)
            for values, into in ((lead, leads), (block - lead, rests)):
                spread = jnp.concatenate(
                    [
                        jnp.broadcast_to(values[r : r + 1], (per_row, LANES))
                        for r in range(step_rows)
                    ],
                    axis=0,
                )
                into.append(jnp.where(mine, spread, 0.0).astype(jnp.bfloat16))
        lead = jnp.concatenate(leads, axis=1)
        rest = jnp.concatenate(rests, axis=1)
        result = dot(lead, w_lead) + (dot(rest, w_lead) + dot(lead, w_rest))
        frames[section, pl.ds(hop * HOP, HOP), :] = jnp.maximum(result, 0.0).astype(jnp.bfloat16)

    for hop in range(spans - 1):
        encode(0, hop)
    pl.semaphore_wait(barrier, devices - 1)
    send_halo(0).start()
    send_audio.start()
    send_halo(1).start()
    for index in range(4, 9):
        loads[index].wait()
    for index in range(9, OPERANDS):
        loads[index].start()
    near = aligned(group_at * half_hop, half_hop)

    def send_out(section, step):
        other = lax.rem(member + step, members)
        source = lax.rem(me + section * members, devices)
        return pltpu.make_async_remote_copy(
            src_ref=sent.at[section, :, :, pl.ds(aligned(other * share, TILE), share), :],
            dst_ref=taken.at[pl.ds(source * spans, spans)],
            send_sem=out_send.at[section, step],
            recv_sem=out_recv.at[section, step],
            device_id={"span": group_at * members + other},
            device_id_type=MESH,
        )

    def do_section(section, _):
        source = lax.rem(me + section * members, devices)

        if section == 1:
            send_audio.wait_recv()
            for hop in range(spans - 1):
                encode(1, hop)

        send_halo(section).wait_recv()

        halo = samples[section, rows:]
        samples[section, rows:] = jnp.where(source == devices - 1, jnp.zeros_like(halo), halo)
        encode(section, spans - 1)
        encode(section, spans)
        starts = []
        for index in range(spans):
            start = frames[section, pl.ds(index * HOP, K), :].astype(jnp.float32)
            start = round_rows(start + table_span[...])
            values = norm_wide(start).astype(jnp.bfloat16)
            normed[index] = values.reshape(K // HOP, HOP, width)
            for half in range(K // HOP):
                at = aligned(index * HOP + half * HOP + near, half_hop)
                start = frames[section, pl.ds(at, half_hop), :].astype(jnp.float32)
                at = aligned(half * HOP + near, half_hop)
                starts.append(round_rows(start + table_span[pl.ds(at, half_hop), :]))
        pair = dot(normed[...].reshape(spans * K, width), intra_kv[...]).astype(jnp.bfloat16)
        mine_normed = normed[:, :, pl.ds(near, half_hop), :].reshape(spans * HOP, width)
        query = query_rows(mine_normed, intra_query)
        mixed = [
            attend_rows(
                query[index * HOP : (index + 1) * HOP],
                pair[index * K : (index + 1) * K, :width],
                pair[index * K : (index + 1) * K, width:],
                None,
            )
            for index in range(spans)
        ]
        result = rest_rows(
            jnp.concatenate(starts, axis=0), jnp.concatenate(mixed, axis=0), *intra_rest
        )
        result = result.astype(jnp.bfloat16)
        sent[section] = result.reshape(spans, K // HOP, half_hop, width)
        for step in range(1, members):
            send_out(section, step).start()
        at = aligned(member * share, TILE)
        taken[pl.ds(source * spans, spans)] = sent[section, :, :, pl.ds(at, share), :]
        return 0

    for section in range(2):
        do_section(section, 0)

    for index in range(9, OPERANDS):
        loads[index].wait()

    def place(source):
        for index in range(spans):
            row = source * spans + index
            block = taken[row].reshape(owned, width).astype(jnp.float32)
            at = aligned(row * owned, owned)
            block = round_rows(block + table_across[pl.ds(row, 1), :])
            for side in range(width // LANES):
                across[side, pl.ds(at, owned), :] = block[:, side * LANES : (side + 1) * LANES]

    def place_section(section, _):
        place(lax.rem(me + section * members, devices))
        for step in range(1, members):
            send_out(section, step).wait_recv()
            other = group_at * members + lax.rem(member + members - step, members)
            place(lax.rem(other + section * members, devices))
        return 0

    for section in range(2):
        place_section(section, 0)

    def send_back(chunk, step):
        other = lax.rem(me + step, devices)
        size = spans * part
        return pltpu.make_async_remote_copy(
            src_ref=back.at[chunk, pl.ds(aligned(other * size, TILE), size), :],
            dst_ref=got.at[chunk, me],
            send_sem=back_send.at[chunk, step],
            recv_sem=back_recv.at[chunk, step],
            device_id={"span": other},
            device_id_type=MESH,
        )

    def do_chunk(chunk, _):
        firsts = [half * share + chunk * part for half in range(2)]
        block = jnp.concatenate(
            [strided(across, first + p, total, owned) for first in firsts for p in range(part)],
            axis=0,
        )
        result = round_rows(layer_rows(block, group, bias, *inter_weights))
        size = part * total
        for half, first in enumerate(firsts):
            at = aligned(first * total, size)
            for side in range(width // LANES):
                inter[side, pl.ds(at, size), :] = result[
                    half * size : (half + 1) * size, side * LANES : (side + 1) * LANES
                ]
        near = chunk * part * total
        far = (share + chunk * part) * total
        pieces = []
        for span in range(total):
            piece = strided(inter, near + span, part, total)
            if span > 0:
                piece = piece + strided(inter, far + span - 1, part, total)
            pieces.append(piece)
        back[chunk] = jnp.concatenate(pieces, axis=0).astype(jnp.bfloat16)
        for step in range(1, devices):
            send_back(chunk, step).start()
        size = spans * part
        got[chunk, me] = back[chunk, pl.ds(aligned(me * size, TILE), size), :]
        return 0

    for chunk in range(chunks):
        do_chunk(chunk, 0)

    def collect(source):
        pieces = [
            got[chunk, source].astype(jnp.float32).reshape(spans, part, width)
            for chunk in range(chunks)
        ]
        summed = jnp.concatenate(pieces, axis=1).reshape(spans * share, width)
        mask = jnp.maximum(dot(summed.astype(jnp.bfloat16), w_mask[...]), 0.0)
        at = aligned(source * share, TILE)
        enc = [frames[0, pl.ds(span * HOP + at, share), :] for span in range(spans)]
        enc = jnp.concatenate(enc, axis=0).astype(jnp.float32)
        out = mask * jnp.concatenate([enc] * SPK, axis=1)
        out = out.astype(jnp.bfloat16).reshape(spans, share, SPK * width)
        out_ref[:, pl.ds(at, share), :] = out

    collect(me)
    for step in range(1, devices):
        for chunk in range(chunks):
            send_back(chunk, step).wait_recv()
        collect(lax.rem(me + devices - step, devices))

    def drain_back(chunk, _):
        for step in range(1, devices):
            send_back(chunk, step).wait_send()
        return 0

    send_audio.wait_send()
    for section in range(2):
        send_halo(section).wait_send()
        for step in range(1, members):
            send_out(section, step).wait_send()
    for chunk in range(chunks):
        drain_back(chunk, 0)


def kernel_body(devices, audio, w_enc, *weights):
    width = w_enc.shape[1]
    rows = audio.shape[0] // LANES
    count = audio.shape[0] // STRIDE
    spans = count // HOP
    total = spans * devices
    share = HOP // devices
    chunks = 2
    part = share // chunks
    group = LANES
    operands = (
        audio.reshape(rows, LANES),
        w_enc,
        position_values(K, width),
        position_values(total, width),
        *weights,
    )
    vmem = pl.BlockSpec(memory_space=pltpu.VMEM)
    far = pl.BlockSpec(memory_space=pl.ANY)
    dma = pltpu.SemaphoreType.DMA
    separated = pl.pallas_call(
        functools.partial(separator_kernel, devices, group),
        out_shape=jax.ShapeDtypeStruct((spans, HOP, SPK * width), jnp.bfloat16),
        in_specs=[far] * len(operands),
        out_specs=vmem,
        scratch_shapes=[
            pltpu.VMEM((2, rows + 2 * HOP * STRIDE // LANES, LANES), jnp.float32),
            *[pltpu.VMEM(operand.shape, operand.dtype) for operand in operands[1:]],
            pltpu.VMEM((2, count + HOP, width), jnp.bfloat16),
            pltpu.VMEM((spans, K // HOP, HOP, width), jnp.bfloat16),
            pltpu.VMEM((2, spans, K // HOP, HOP // 2, width), jnp.bfloat16),
            pltpu.VMEM((total, K // HOP, share, width), jnp.bfloat16),
            pltpu.VMEM((width // LANES, total * 2 * share, LANES), jnp.float32),
            pltpu.VMEM((width // LANES, total * 2 * share, LANES), jnp.float32),
            pltpu.VMEM((chunks, total * part, width), jnp.bfloat16),
            pltpu.VMEM((chunks, devices, spans * part, width), jnp.bfloat16),
            dma,
            dma,
            dma((2,)),
            dma((2,)),
            dma((2, devices // 2)),
            dma((2, devices // 2)),
            dma((chunks, devices)),
            dma((chunks, devices)),
            dma((len(operands),)),
        ],
        compiler_params=pltpu.CompilerParams(
            collective_id=0, has_side_effects=True, vmem_limit_bytes=60 * 2**20
        ),
    )(*operands)
    return separated.reshape(count, SPK * width)


def fits_kernel(devices, count):
    spans = count // HOP
    share = HOP // devices
    return (
        HOP % devices == 0
        and share % TILE == 0
        and LANES % (spans * devices) == 0
        and share * (devices // 2) == HOP // 2
        and spans >= 4
        and spans % 2 == 0
        and devices % 2 == 0
    )


def body(audio, w_enc, *weights):
    devices = lax.axis_size("span")
    if fits_kernel(devices, audio.shape[0] // STRIDE):
        return kernel_body(devices, audio, w_enc, *weights)
    return plain_body(audio, w_enc, *weights)


def solution(mesh):
    placed = (P(("mix", "span")), P(), P(), P(), P(), P(), P(), P(), P(), P(), P(), P(), P())
    return jax.shard_map(
        body, mesh=mesh, in_specs=placed, out_specs=P(("mix", "span"), None), check_vma=False
    )
```
